512 devices in a mesh: row: 16 (over x, y), col: 32 (over z, core).
Axes of the slice: x: 4, y: 4, z: 16, core: 2. Of those that a mesh axis runs over, the one named last changes fastest.
Arguments:
- frames: bfloat16 [131072, 440], P(('row', 'col')), may hold values from -7 to 7
- labels: bfloat16 [131072, 147], P(('row', 'col')), may hold values from -6 to 6
- weights: float32 [131072, 147], P(('row', 'col')), may hold values from -0.0625 to 0.0625
- picks: int32 [2, 512], replicated, may hold values from 0 to 255, as said below
Outputs:
- updated: float32 [131072, 147], P(('row', 'col'))
The draws below stay inside these ranges and needn't reach their ends.
Inputs may be any that keep to these rules, and one draw needn't show every extreme that they name: `picks`: device d owns the 1 block positions j with j == d; within one step, the frame indices at one device's positions are all different.
All inputs are finite; a program needn't handle non-finite values.
Results may differ from the reference program's by a relative error of at most 0.0005.
Values may be sent and summed in bfloat16 or wider, within the bound.
No kernel may reach another device: no remote copies, remote signals or barrier semaphores. Data moves between devices by JAX's collectives and lax.ppermute only.
A program may use at most 64 MiB of HBM per device.

```python
import math
import jax
import jax.numpy as jnp
from jax import lax

FEATS = 440
TARGETS = 147
BLOCK = 512
STEPS = 2
ROWS_DEV = 256
ROWS = 131072
N_ROW = 16
N_COL = 32


def draw_frames(key, part):
    key = jax.random.fold_in(key, 11)
    centre_key, member_key, noise_key, level_key, size_key = jax.random.split(key, 5)
    centre_count = 128
    members = jax.random.randint(member_key, (ROWS,), 0, centre_count, jnp.int32)
    centres = jnp.clip(jax.random.normal(centre_key, (centre_count, FEATS), jnp.float32), -4.0, 4.0)
    noise = jnp.clip(jax.random.normal(noise_key, (ROWS, FEATS), jnp.float32), -4.0, 4.0)
    levels = jnp.exp(jax.random.uniform(level_key, (ROWS, 1), jnp.float32, math.log(0.3), math.log(0.5)))
    centre_scales = jnp.exp(jax.random.uniform(size_key, (centre_count, 1), jnp.float32, math.log(0.85), math.log(1.2)))
    values = (centres * centre_scales)[members] + levels * noise
    return jnp.clip(values, -6.9, 6.9).astype(jnp.bfloat16)


def draw_picks(key, part):
    key = jax.random.fold_in(key, 23)
    devices = N_ROW * N_COL
    per_device = BLOCK // devices
    scores = jax.random.randint(key, (STEPS, devices, ROWS_DEV), 0, 2 ** 18, jnp.int32)
    scores = scores * ROWS_DEV + jnp.arange(ROWS_DEV, dtype=jnp.int32)
    scores = scores.at[0, 0, ROWS_DEV - 1].set(-2)
    scores = scores.at[0, devices - 1, 0].set(-1)
    chosen = jnp.argsort(scores, axis=-1)[:, :, :per_device]
    return chosen.reshape(STEPS, devices * per_device).astype(jnp.int32)


def block_levels(own_key, extent, shards, low, top_value):
    factor_of, own = 1.0, jax.random.fold_in(own_key, 6)
    for position, parts in shards:
        steps = jnp.exp(jax.random.uniform(jax.random.fold_in(own, position), (parts,), jnp.float32, low / len(shards), top_value / len(shards)))
        factor_of = factor_of * jnp.repeat(steps, extent[position] // parts).reshape([-1 if axis == position else 1 for axis in range(len(extent))])
    return factor_of


def normal_values(own_key, dims, spread, most, shards=(), kind=jnp.bfloat16):
    drawn = spread * jax.random.normal(own_key, dims, jnp.float32)
    if shards:
        drawn = drawn * block_levels(own_key, dims, shards, -0.22, 0.18)
    return jnp.clip(drawn, -most, most).astype(kind)


def setup_inputs(seed: int = 0) -> dict:
    splits = jax.random.split(jax.random.key(seed), 5)
    return {
        "frames": draw_frames(jax.random.fold_in(splits[4], 71), 0),
        "labels": normal_values(splits[1], (ROWS, TARGETS), 1.0, 6.0, ((0, 512),)),
        "weights": normal_values(splits[2], (ROWS, TARGETS), (ROWS // 16) ** -0.5, 0.0625, ((0, 512),), jnp.float32),
        "picks": draw_picks(jax.random.fold_in(splits[4], 71), 0),
    }


ridge = 1.0

def kernel_of(first_rows, second_rows):
    first_wide = first_rows.astype(jnp.float32)
    second_wide = second_rows.astype(jnp.float32)
    inner_products = jnp.dot(first_wide, second_wide.T, precision=lax.Precision.HIGHEST)
    first_sq = jnp.sum(first_wide * first_wide, axis=1)
    second_sq = jnp.sum(second_wide * second_wide, axis=1)
    width = first_rows.shape[1]
    return jnp.exp(-(first_sq[:, None] + second_sq[None, :] - 2.0 * inner_products) * (0.5 / width))

def contract(kernel_rows, weight_rows):
    return lax.dot_general(kernel_rows.astype(jnp.float32), weight_rows.astype(jnp.float32), (((0,), (0,)), ((), ())), precision=lax.Precision.HIGHEST, preferred_element_type=jnp.float32)

def solve_block(gram, rhs):
    factor = jnp.linalg.cholesky(gram)
    middle = lax.linalg.triangular_solve(factor, rhs, left_side=True, lower=True)
    return lax.linalg.triangular_solve(factor, middle, left_side=True, lower=True, transpose_a=True)

def reference(frames, labels, weights, picks):
    devices = N_ROW * N_COL
    per_device = BLOCK // devices
    owners = (jnp.arange(BLOCK, dtype=jnp.int32) // per_device).astype(jnp.int32)
    identity = jnp.eye(BLOCK, dtype=jnp.float32)
    current = weights
    for iteration in range(STEPS):
        global_ids = (owners * ROWS_DEV + picks[iteration]).astype(jnp.int32)
        block_frames = frames[global_ids]

        def add_shard(totals, shard_index):
            begin = (shard_index * ROWS_DEV).astype(jnp.int32)
            shard_rows = lax.dynamic_slice_in_dim(frames, begin, ROWS_DEV, 0)
            weight_rows = lax.dynamic_slice_in_dim(current, begin, ROWS_DEV, 0)
            near_kernel = kernel_of(shard_rows, block_frames)
            return (totals + contract(near_kernel, weight_rows), None)
        kernel_sums, unused = lax.scan(add_shard, jnp.zeros((BLOCK, TARGETS), jnp.float32), jnp.arange(devices, dtype=jnp.int32))
        rhs = labels[global_ids].astype(jnp.float32) - ridge * current[global_ids] - kernel_sums
        gram = kernel_of(block_frames, block_frames) + ridge * identity
        delta = solve_block(gram, rhs)
        current = current.at[global_ids].add(delta)
    return current
```

```python
import functools

import jax
import jax.numpy as jnp
from jax import lax
from jax.experimental import pallas as pl
from jax.experimental.pallas import tpu as pltpu
from jax.sharding import Mesh, PartitionSpec as P

RIDGE = 1.0
LANES = 128
NEWTON_STEPS = 6
VMEM_BYTES = 48 * 1024 * 1024

NT = (((1,), (1,)), ((), ()))
NN = (((1,), (0,)), ((), ()))
TN = (((0,), (0,)), ((), ()))


def mm(a, b, dims=NN):
    return lax.dot_general(a, b, dims, preferred_element_type=jnp.float32)


def split(a):
    hi = a.astype(jnp.bfloat16)
    lo = (a - hi.astype(jnp.float32)).astype(jnp.bfloat16)
    return hi, lo


def mm3(a, b, dims=NN):
    return mm(a[0], b[0], dims) + (mm(a[0], b[1], dims) + mm(a[1], b[0], dims))


def mm6(a, b, dims=NN):
    return lax.dot_general(
        a, b, dims, precision=lax.Precision.HIGHEST, preferred_element_type=jnp.float32
    )


def eye_mask(n):
    return lax.broadcasted_iota(jnp.int32, (n, n), 0) == lax.broadcasted_iota(jnp.int32, (n, n), 1)


def inverses(mats):
    n = mats[0].shape[0]
    eye = jnp.where(eye_mask(n), 1.0, 0.0).astype(jnp.float32)
    state = []
    for a in mats:
        top = jnp.maximum(jnp.max(jnp.sum(jnp.abs(a), axis=1, keepdims=True), axis=0, keepdims=True), 1.5)
        scale = 2.0 / (1.0 + top)
        err = (top - 1.0) / (top + 1.0)
        gain = 2.0 / (2.0 - err * err)
        x = (gain * scale) * (2.0 * eye - scale * a)
        err = err * err * gain * 0.5
        state.append((a, split(a), x, err))
    for step in range(NEWTON_STEPS):
        later = []
        for a, parts, x, err in state:
            gain = 2.0 / (2.0 - err * err)
            if step < NEWTON_STEPS - 1:
                xs = split(x)
                y = mm3(parts, xs)
                x = gain * (2.0 * x - mm3(xs, split(y)))
            else:
                r = eye - mm6(a, x)
                x = gain * (x + mm3(split(x), split(r)))
            err = err * err * gain * 0.5
            later.append((a, parts, x, err))
        state = later
    return [s[2] for s in state]


def factor(grams):
    h = grams[0].shape[0] // 2
    firsts = inverses([g[:h, :h] for g in grams])
    couples = [mm6(x, g[:h, h:]) for x, g in zip(firsts, grams)]
    schurs = [g[h:, h:] - mm6(g[h:, :h], u) for g, u in zip(grams, couples)]
    seconds = inverses(schurs)
    return list(zip(firsts, couples, seconds, [g[h:, :h] for g in grams]))


def solve(parts, t):
    first, couple, second, lower = parts
    h = first.shape[0]
    y = mm6(first, t[:h])
    z = mm6(second, t[h:] - mm6(lower, y))
    return jnp.concatenate([y - mm6(couple, z), z], axis=0)


def pick_kernel(scal_ref, f0_ref, f1_ref, out_ref):
    feats = f0_ref.shape[1]
    rows = f0_ref.shape[0]
    for s, ref in enumerate((f0_ref, f1_ref)):
        at = scal_ref[s] % rows
        mask = lax.broadcasted_iota(jnp.int32, (rows, feats), 0) == at
        row = jnp.sum(jnp.where(mask, ref[...].astype(jnp.float32), 0.0), axis=0, keepdims=True)
        for c in range(4):
            lo = c * LANES
            wide = min(LANES, feats - lo)
            piece = row[:, lo : lo + wide]
            if wide < LANES:
                piece = jnp.concatenate([piece, jnp.zeros((1, LANES - wide), jnp.float32)], axis=1)
            out_ref[s * 4 + c : s * 4 + c + 1, :] = piece


def main_kernel(scal_ref, mine_ref, other_ref, frames_ref, sq_ref, weights_ref, labels_ref, same_ref, out_ref, wide_ref, lab_ref):
    rows, feats = frames_ref.shape
    targets = weights_ref.shape[1]
    half = mine_ref.shape[0]
    block = 2 * half
    factor_ = 0.5 / feats
    core = scal_ref[2]
    pos = scal_ref[3]
    mine = mine_ref[...]
    other = other_ref[...]
    flip = core == 0
    first = jnp.where(flip, mine, other)
    second = jnp.where(flip, other, mine)
    both = jnp.concatenate([first, second], axis=0)
    width = both.shape[1] // 2
    chosen = [both[:, :width], both[:, width:]]

    wide_ref[...] = jnp.zeros_like(wide_ref)
    wide_ref[:, :targets] = weights_ref[...]
    lab_ref[...] = jnp.zeros_like(lab_ref)
    lab_ref[:, :targets] = labels_ref[...].astype(jnp.float32)
    weights = wide_ref[...]
    frames = frames_ref[...]

    diag = eye_mask(block)
    inner = [mm(c, c, NT) for c in chosen]
    cross = mm(chosen[1], chosen[0], NT)
    tall = [jnp.sum(jnp.where(diag, g, 0.0), axis=1, keepdims=True) for g in inner]
    flat = [jnp.sum(jnp.where(diag, g, 0.0), axis=0, keepdims=True) for g in inner]
    one = jnp.where(diag, RIDGE, 0.0)
    grams = [jnp.exp(-(tall[s] + flat[s] - 2.0 * inner[s]) * factor_) + one for s in range(2)]
    between = jnp.exp(-(tall[1] + flat[0] - 2.0 * cross) * factor_)
    between = between + jnp.where(diag, RIDGE * same_ref[...], 0.0)

    here = lax.broadcasted_iota(jnp.int32, (block, 1), 0) == pos
    own = lab_ref[...] - RIDGE * weights
    at = lax.broadcasted_iota(jnp.int32, (rows, 1), 0)
    wsplit = split(weights)
    terms = []
    for s in range(2):
        near = jnp.exp(-(tall[s] + sq_ref[...] - 2.0 * mm(chosen[s][:, :feats], frames, NT)) * factor_)
        picked = jnp.sum(jnp.where(at == scal_ref[s], own, 0.0), axis=0, keepdims=True)
        terms.append(jnp.where(here, picked, 0.0) - mm3(split(near), wsplit))

    parts = factor(grams)
    delta0 = solve(parts[0], terms[0])
    delta1 = solve(parts[1], terms[1] - mm6(between, delta0))

    per = 16
    groups = half // per
    packed = None
    for s, d in enumerate((delta0, delta1)):
        body = d[:, :LANES].reshape(2, groups, per, LANES)
        rest = d[:, LANES:].reshape(2 * groups, 2, 8, LANES)
        for c in range(2):
            out_ref[:, c, s * per : (s + 1) * per, :] = body[c]
        for g in range(2):
            piece = rest[:, g].reshape(2 * groups * 8, LANES)
            turn = (2 * s + g) * 32
            if turn:
                piece = pltpu.roll(piece, turn, 1)
            packed = piece if packed is None else packed + piece
    packed = packed.reshape(2, groups, 8, LANES)
    for c in range(2):
        out_ref[:, c, 2 * per :, :] = packed[c]


def mid_kernel(got_ref, out_ref):
    total = jnp.sum(got_ref[...], axis=0)
    per = 16
    rest = total[2 * per :]
    for s in range(2):
        out_ref[:, s, :] = total[s * per : (s + 1) * per]
        halves = []
        for g in range(2):
            turn = (2 * s + g) * 32
            piece = pltpu.roll(rest, LANES - turn, 1) if turn else rest
            halves.append(piece)
        out_ref[:, 2 + s, :] = jnp.concatenate(halves, axis=0)


def end_kernel(scal_ref, got_ref, weights_ref, out_ref):
    rows, targets = weights_ref.shape
    total = jnp.sum(got_ref[...], axis=0)
    at = lax.broadcasted_iota(jnp.int32, (rows, 1), 0)
    out = weights_ref[...]
    for s in range(2):
        delta = jnp.concatenate([total[s : s + 1], total[2 + s : 3 + s]], axis=1)[:, :targets]
        out = out + jnp.where(at == scal_ref[s], delta, 0.0)
    out_ref[...] = out


def params():
    return pltpu.CompilerParams(vmem_limit_bytes=VMEM_BYTES)


VMEM = pl.BlockSpec(memory_space=pltpu.VMEM)
SMEM = pl.BlockSpec(memory_space=pltpu.SMEM)


def shards(frames, labels, weights, picks):
    rows, feats = frames.shape
    targets = weights.shape[1]
    n_xy, n_z, n_core = (lax.axis_size(a) for a in ("xy", "z", "core"))
    block = picks.shape[1]
    half = block // 2
    xy, z, core = (lax.axis_index(a) for a in ("xy", "z", "core"))
    device = (xy * n_z + z) * n_core + core
    pos = core * half + xy * n_z + z
    mine = lax.dynamic_slice(picks, (0, device), (2, 1)).reshape(2)
    scal = jnp.concatenate([mine, jnp.stack([core, pos]).astype(jnp.int32)])

    rowspec = lambda s: pl.BlockSpec((16, feats), lambda i, scal_ref: (scal_ref[s] // 16, 0))
    chosen = pl.pallas_call(
        pick_kernel,
        grid_spec=pltpu.PrefetchScalarGridSpec(
            num_scalar_prefetch=1,
            grid=(1,),
            in_specs=[rowspec(0), rowspec(1)],
            out_specs=pl.BlockSpec((8, LANES), lambda i, scal_ref: (0, 0)),
        ),
        out_shape=jax.ShapeDtypeStruct((8, LANES), jnp.float32),
    )(scal, frames, frames).astype(jnp.bfloat16)

    got = lax.all_to_all(jnp.broadcast_to(chosen[None], (n_z, 8, LANES)), "z", 0, 0)
    got = got.reshape(n_z, 8 * LANES)
    got = lax.all_to_all(jnp.broadcast_to(got[None], (n_xy,) + got.shape), "xy", 0, 0)
    got = got.reshape(half, 8 * LANES)
    other = lax.ppermute(got, "core", [(0, 1), (1, 0)])

    wide = frames.astype(jnp.float32)
    squares = jnp.sum(wide * wide, axis=1)[None, :]
    same = (picks[0] == picks[1]).astype(jnp.float32)
    same = same.reshape(n_xy * n_z, n_core).T.reshape(1, block)

    sent = pl.pallas_call(
        main_kernel,
        in_specs=[SMEM] + [VMEM] * 7,
        out_specs=VMEM,
        out_shape=jax.ShapeDtypeStruct((n_xy, n_core, 40, LANES), jnp.float32),
        scratch_shapes=[pltpu.VMEM((rows, 2 * LANES), jnp.float32)] * 2,
        compiler_params=params(),
    )(scal, got, other, frames, squares, weights, labels, same)

    got = lax.all_to_all(sent.reshape(n_xy * n_core, 40, LANES), ("xy", "core"), 0, 0)
    part = pl.pallas_call(
        mid_kernel,
        in_specs=[VMEM],
        out_specs=VMEM,
        out_shape=jax.ShapeDtypeStruct((n_z, 4, LANES), jnp.float32),
        compiler_params=params(),
    )(got)
    got = lax.all_to_all(part, "z", 0, 0)
    return pl.pallas_call(
        end_kernel,
        in_specs=[SMEM, VMEM, VMEM],
        out_specs=VMEM,
        out_shape=jax.ShapeDtypeStruct((rows, targets), jnp.float32),
        compiler_params=params(),
    )(scal, got, weights)


def solution(mesh):
    grid = Mesh(mesh.devices.reshape(mesh.shape["row"], -1, 2), ("xy", "z", "core"))
    spread = P(("xy", "z", "core"), None)
    return jax.shard_map(
        shards, mesh=grid, in_specs=(spread, spread, spread, P()), out_specs=spread, check_vma=False
    )
```

```python
import jax
import jax.numpy as jnp
from jax import lax
from jax.experimental import pallas as pl
from jax.experimental.pallas import tpu as pltpu
from jax.sharding import Mesh, PartitionSpec as P

RIDGE = 1.0
LANES = 128
JOINT_STEPS = 3
VMEM_BYTES = 40 * 1024 * 1024

NN = (((1,), (0,)), ((), ()))
NT = (((1,), (1,)), ((), ()))


def mm(a, b, dims=NN):
    return lax.dot_general(a, b, dims, preferred_element_type=jnp.float32)


def mm6(a, b, dims=NN):
    return lax.dot_general(
        a, b, dims, precision=lax.Precision.HIGHEST, preferred_element_type=jnp.float32
    )


def split(a):
    hi = a.astype(jnp.bfloat16)
    lo = (a - hi.astype(jnp.float32)).astype(jnp.bfloat16)
    return hi, lo


def mm3(a, b, dims=NN):
    rows = a[0].shape[0]
    left = mm(jnp.concatenate(a, axis=0), b[0], dims)
    return left[:rows] + (left[rows:] + mm(a[0], b[1], dims))


def eye_mask(n):
    return lax.broadcasted_iota(jnp.int32, (n, n), 0) == lax.broadcasted_iota(jnp.int32, (n, n), 1)


def inverses(mats):
    n = mats[0].shape[0]
    eye = jnp.where(eye_mask(n), 1.0, 0.0).astype(jnp.float32)
    state = []
    for a in mats:
        top = jnp.max(jnp.sum(jnp.abs(a), axis=0, keepdims=True), axis=1, keepdims=True)
        top = jnp.maximum(top, 1.5)
        scale = 2.0 / (1.0 + top)
        err = (top - 1.0) / (top + 1.0)
        gain = 2.0 / (2.0 - err * err)
        r = eye - scale * a
        x = (gain * scale) * (eye + r)
        rs = split(r)
        r = (1.0 - gain) * eye + gain * mm3(rs, rs)
        state.append((x, r, err * err * gain * 0.5))
    for step in range(JOINT_STEPS + 1):
        later = []
        for x, r, err in state:
            gain = 2.0 / (2.0 - err * err)
            rs = split(r)
            xs = split(x)
            if step < JOINT_STEPS:
                left = mm(jnp.concatenate(xs + rs, axis=0), rs[0])
                square = left[2 * n : 3 * n] + (left[3 * n :] + mm(rs[0], rs[1]))
                r = (1.0 - gain) * eye + gain * square
            else:
                left = mm(jnp.concatenate(xs, axis=0), rs[0])
            x = gain * (x + (left[:n] + left[n : 2 * n]))
            later.append((x, r, err * err * gain * 0.5))
        state = later
    for last in (False, True):
        later = []
        for a, (x, r, err) in zip(mats, state):
            gain = 2.0 / (2.0 - err * err)
            xs = split(x)
            r = eye - (mm6(a, x) if last else mm3(split(a), xs))
            left = mm(jnp.concatenate(xs, axis=0), r.astype(jnp.bfloat16))
            x = gain * (x + (left[:n] + left[n:]))
            later.append((x, r, err * err * gain * 0.5))
        state = later
    return [s[0] for s in state]


def place():
    xy, z, core = (lax.axis_index(a) for a in ("xy", "z", "core"))
    n_z, n_core = lax.axis_size("z"), lax.axis_size("core")
    return (xy * n_z + z) * n_core + core, xy * n_z + z, core


def onehots(picks_ref, device, rows):
    at = lax.broadcasted_iota(jnp.int32, (8, rows), 1)
    row = lax.broadcasted_iota(jnp.int32, (8, rows), 0)
    want = jnp.where(row == 0, picks_ref[0, device], jnp.where(row == 1, picks_ref[1, device], -1))
    return jnp.where(at == want, 1.0, 0.0)


def pick_kernel(picks_ref, frames_ref, out_ref):
    feats, rows = frames_ref.shape
    device, _, _ = place()
    chosen = mm(onehots(picks_ref, device, rows).astype(jnp.bfloat16), frames_ref[...], NT)
    same = jnp.where(picks_ref[0, device] == picks_ref[1, device], 1.0, 0.0)
    lane = lax.broadcasted_iota(jnp.int32, (1, LANES), 1)
    parts = []
    for s in range(2):
        for c in range(4):
            lo = c * LANES
            wide = min(LANES, feats - lo)
            piece = chosen[s : s + 1, lo : lo + wide]
            if wide < LANES:
                piece = jnp.concatenate([piece, jnp.zeros((1, LANES - wide), jnp.float32)], axis=1)
                piece = jnp.where(lane == wide, same, piece)
            parts.append(piece)
    row = jnp.concatenate(parts, axis=0).astype(jnp.bfloat16)
    out_ref[...] = jnp.broadcast_to(row[None], out_ref.shape)


def halves(ref, feats):
    width = ref.shape[1] // 2
    return [ref[:, s * width : s * width + feats] for s in range(2)]


def gauss(tall, flat, inner, feats):
    return jnp.exp(-(tall + flat - 2.0 * inner) * (0.5 / feats))


def diag_sums(inner, diag):
    masked = jnp.where(diag, inner, 0.0)
    return jnp.sum(masked, axis=1, keepdims=True), jnp.sum(masked, axis=0, keepdims=True)


def term_of(chosen, tall, frames, frame_sq, wsplit, feats):
    near = gauss(tall, frame_sq, mm(chosen, frames), feats)
    return mm3(wsplit, split(near), NT)


def frame_squares(frames):
    wide = frames.astype(jnp.float32)
    return jnp.sum(wide * wide, axis=0, keepdims=True)


def padded(ref, scratch):
    scratch[...] = jnp.zeros_like(scratch)
    scratch[: ref.shape[0], :] = ref[...].astype(jnp.float32)
    return scratch[...]


def own_kernel(picks_ref, own_ref, frames_ref, weights_ref, labels_ref, inv_ref, term_ref, tall_ref, flat_ref, w_scr, l_scr):
    feats, rows = frames_ref.shape
    half = own_ref.shape[0]
    device, pos, _ = place()
    chosen = halves(own_ref, feats)
    diag = eye_mask(half)
    one = jnp.where(diag, RIDGE, 0.0)
    inner = [mm(c, c, NT) for c in chosen]
    sums = [diag_sums(g, diag) for g in inner]
    mats = [gauss(t, f, g, feats) + one for (t, f), g in zip(sums, inner)]
    inv = inverses(mats)
    for s in range(2):
        inv_ref[s] = inv[s]
        flat_ref[s : s + 1, :] = sums[s][1]
        tall_ref[:, s : s + 1] = sums[s][0]
    frames = frames_ref[...]
    frame_sq = frame_squares(frames)
    weights = padded(weights_ref, w_scr)
    wsplit = split(weights)
    start = padded(labels_ref, l_scr) - RIDGE * weights
    hot = onehots(picks_ref, device, rows)
    here = lax.broadcasted_iota(jnp.int32, (1, half), 1) == pos
    for s in range(2):
        picked = jnp.sum(start * hot[s : s + 1], axis=1, keepdims=True)
        term = term_of(chosen[s], sums[s][0], frames, frame_sq, wsplit, feats)
        term_ref[s] = jnp.where(here, picked, 0.0) - term


def rest_kernel(own_ref, other_ref, frames_ref, weights_ref, inv_ref, term_ref, tall_ref, flat_ref, out_ref, w_scr):
    feats, rows = frames_ref.shape
    half = own_ref.shape[0]
    _, _, core = place()
    near = halves(own_ref, feats)
    far = halves(other_ref, feats)
    diag = eye_mask(half)
    one = jnp.where(diag, RIDGE, 0.0)
    inner = [mm(c, c, NT) for c in far]
    sums = [diag_sums(g, diag) for g in inner]
    talls = [[tall_ref[:, s : s + 1], sums[s][0]] for s in range(2)]
    flats = [[flat_ref[s : s + 1, :], sums[s][1]] for s in range(2)]
    chosen = [[near[s], far[s]] for s in range(2)]

    def block(s, i, t, j):
        return gauss(talls[s][i], flats[t][j], mm(chosen[s][i], chosen[t][j], NT), feats)

    inv, couple, lower, upper, schur = [], [], [], [], []
    for s in range(2):
        inv.append(inv_ref[s])
        upper.append(block(s, 0, s, 1))
        lower.append(block(s, 1, s, 0))
        couple.append(mm6(inv[s], upper[s]))
        corner = gauss(talls[s][1], flats[s][1], inner[s], feats) + one
        schur.append(corner - mm6(lower[s], couple[s]))
    inv2 = inverses(schur)

    frames = frames_ref[...]
    frame_sq = frame_squares(frames)
    wsplit = split(padded(weights_ref, w_scr))
    width = own_ref.shape[1] // 2
    flags = [r[:, width + feats : width + feats + 1].astype(jnp.float32) for r in (own_ref, other_ref)]
    deltas = []
    for s in range(2):
        first = term_ref[s]
        second = -term_of(far[s], talls[s][1], frames, frame_sq, wsplit, feats)
        if s == 1:
            cross = [[block(1, i, 0, j) for j in range(2)] for i in range(2)]
            for i in range(2):
                cross[i][i] = cross[i][i] + jnp.where(diag, RIDGE * flags[i], 0.0)
            first = first - (mm6(deltas[0][0], cross[0][0], NT) + mm6(deltas[0][1], cross[0][1], NT))
            second = second - (mm6(deltas[0][0], cross[1][0], NT) + mm6(deltas[0][1], cross[1][1], NT))
        y = mm6(first, inv[s])
        z = mm6(second - mm6(y, upper[s]), inv2[s])
        deltas.append((y - mm6(z, couple[s], NT), z))

    per = 16
    groups = half // per
    fill = jnp.zeros((2 * LANES - deltas[0][0].shape[0], half), jnp.float32)
    for i, slot in enumerate((core, 1 - core)):
        packed = None
        for s in range(2):
            full = jnp.concatenate([deltas[s][i], fill], axis=0)
            body = jnp.transpose(full[:LANES])
            out_ref[:, pl.ds(slot, 1), s * per : (s + 1) * per, :] = body.reshape(groups, 1, per, LANES)
            tail = jnp.transpose(full[LANES:]).reshape(groups, 2, 8, LANES)
            for g in range(2):
                piece = tail[:, g].reshape(groups * 8, LANES)
                turn = (2 * s + g) * 32
                if turn:
                    piece = pltpu.roll(piece, turn, 1)
                packed = piece if packed is None else packed + piece
        out_ref[:, pl.ds(slot, 1), 2 * per :, :] = packed.reshape(groups, 1, 8, LANES)


def mid_kernel(got_ref, out_ref):
    total = jnp.sum(got_ref[...], axis=0)
    per = 16
    rest = total[2 * per :]
    for s in range(2):
        out_ref[:, s, :] = total[s * per : (s + 1) * per]
        pieces = []
        for g in range(2):
            turn = (2 * s + g) * 32
            pieces.append(pltpu.roll(rest, LANES - turn, 1) if turn else rest)
        out_ref[:, 2 + s, :] = jnp.concatenate(pieces, axis=0)


def end_kernel(picks_ref, got_ref, weights_ref, out_ref):
    targets, rows = weights_ref.shape
    device, _, _ = place()
    total = jnp.sum(got_ref[...], axis=0)
    turned = jnp.transpose(jnp.concatenate([total, jnp.zeros((LANES - 4, LANES), jnp.float32)], axis=0))
    hot = onehots(picks_ref, device, rows)
    out_ref[:LANES, :] = weights_ref[:LANES, :] + (turned[:, 0:1] * hot[0:1] + turned[:, 1:2] * hot[1:2])
    left = targets - LANES
    out_ref[LANES:, :] = weights_ref[LANES:, :] + (
        turned[:left, 2:3] * hot[0:1] + turned[:left, 3:4] * hot[1:2]
    )


VMEM = pl.BlockSpec(memory_space=pltpu.VMEM)
SMEM = pl.BlockSpec(memory_space=pltpu.SMEM)


def kernel(body, ins, outs, scratch=(), flops=0):
    single = not isinstance(outs, list)
    return pl.pallas_call(
        body,
        in_specs=ins,
        out_specs=VMEM if single else [VMEM] * len(outs),
        out_shape=outs,
        scratch_shapes=list(scratch),
        compiler_params=pltpu.CompilerParams(vmem_limit_bytes=VMEM_BYTES),
        cost_estimate=pl.CostEstimate(flops=flops, bytes_accessed=1 << 20, transcendentals=0),
    )


def f32(*dims):
    return jax.ShapeDtypeStruct(dims, jnp.float32)


def update(got, other, frames, weights, labels, picks, n_xy):
    half = got.shape[0]
    targets, rows = weights.shape
    tall = -(-targets // 8) * 8
    scratch = pltpu.VMEM((tall, rows), jnp.float32)
    known = kernel(
        own_kernel,
        [SMEM] + [VMEM] * 4,
        [f32(2, half, half), f32(2, tall, half), f32(half, 2), f32(2, half)],
        [scratch, scratch],
        flops=6_000_000_000,
    )(picks, got, frames, weights, labels)
    return kernel(rest_kernel, [VMEM] * 8, f32(n_xy, 2, 40, LANES), [scratch], flops=6_000_000_000)(
        got, other, frames, weights, *known
    )


def shards(frames, labels, weights, picks):
    n_xy, n_z, n_core = (lax.axis_size(a) for a in ("xy", "z", "core"))
    frames, labels, weights = frames.T, labels.T, weights.T
    sent = kernel(pick_kernel, [SMEM, VMEM], jax.ShapeDtypeStruct((n_z, 8, LANES), jnp.bfloat16))(picks, frames)
    got = lax.all_to_all(sent, "z", 0, 0).reshape(n_z, 8 * LANES)
    got = lax.all_to_all(jnp.broadcast_to(got[None], (n_xy,) + got.shape), "xy", 0, 0)
    got = got.reshape(n_xy * n_z, 8 * LANES)
    other = lax.ppermute(got, "core", [(0, 1), (1, 0)])
    sent = update(got, other, frames, weights, labels, picks, n_xy)
    got = lax.all_to_all(sent.reshape(n_xy * n_core, 40, LANES), ("xy", "core"), 0, 0)
    part = kernel(mid_kernel, [VMEM], f32(n_z, 4, LANES))(got)
    got = lax.all_to_all(part, "z", 0, 0)
    return kernel(end_kernel, [SMEM, VMEM, VMEM], f32(*weights.shape))(picks, got, weights).T


def solution(mesh):
    grid = Mesh(mesh.devices.reshape(mesh.shape["row"], -1, 2), ("xy", "z", "core"))
    spread = P(("xy", "z", "core"), None)
    return jax.shard_map(
        shards, mesh=grid, in_specs=(spread, spread, spread, P()), out_specs=spread, check_vma=False
    )
```

```python
import jax
import jax.numpy as jnp
from jax import lax
from jax.experimental import pallas as pl
from jax.experimental.pallas import tpu as pltpu
from jax.sharding import Mesh, PartitionSpec as P

RIDGE = 1.0
LANES = 128
JOINT_STEPS = 4
VMEM_BYTES = 40 * 1024 * 1024

NN = (((1,), (0,)), ((), ()))
NT = (((1,), (1,)), ((), ()))


def mm(a, b, dims=NN):
    return lax.dot_general(a, b, dims, preferred_element_type=jnp.float32)


def split(a):
    hi = a.astype(jnp.bfloat16)
    lo = (a - hi.astype(jnp.float32)).astype(jnp.bfloat16)
    return hi, lo


def split3(a):
    hi = a.astype(jnp.bfloat16)
    rest = a - hi.astype(jnp.float32)
    mid = rest.astype(jnp.bfloat16)
    return hi, mid, (rest - mid.astype(jnp.float32)).astype(jnp.bfloat16)


def joined(left, right, dims):
    return mm(jnp.concatenate(left, axis=dims[0][0][0]), jnp.concatenate(right, axis=dims[0][1][0]), dims)


def mm3(a, b, dims=NN):
    return joined((a[0], a[1], a[0]), (b[0], b[0], b[1]), dims)


def split(a):
    hi = a.astype(jnp.bfloat16)
    lo = (a - hi.astype(jnp.float32)).astype(jnp.bfloat16)
    return hi, lo


def split3(a):
    hi = a.astype(jnp.bfloat16)
    rest = a - hi.astype(jnp.float32)
    mid = rest.astype(jnp.bfloat16)
    return hi, mid, (rest - mid.astype(jnp.float32)).astype(jnp.bfloat16)


def joined(left, right, dims):
    return mm(jnp.concatenate(left, axis=dims[0][0][0]), jnp.concatenate(right, axis=dims[0][1][0]), dims)


def mm3(a, b, dims=NN):
    return joined((a[0], a[1], a[0]), (b[0], b[0], b[1]), dims)


def mm6(a, b, dims=NN):
    a, b = split3(a), split3(b)
    return joined((a[0], a[1], a[2], a[0], a[1], a[0]), (b[0], b[0], b[0], b[1], b[1], b[2]), dims)


def mm6_rows(a, b, dims=NN):
    n = a.shape[0]
    a, b = split3(a), split3(b)
    p = mm(jnp.concatenate(a, axis=0), b[0], dims)
    q = mm(jnp.concatenate(a[:2], axis=0), b[1], dims)
    return p[:n] + (p[n : 2 * n] + q[:n]) + (p[2 * n :] + q[n:] + mm(a[0], b[2], dims))


def eye_mask(n):
    return lax.broadcasted_iota(jnp.int32, (n, n), 0) == lax.broadcasted_iota(jnp.int32, (n, n), 1)


def inverses(mats, others=()):
    others = list(others)

    def between():
        if others:
            others.pop(0)()

    n = mats[0].shape[0]
    eye = jnp.where(eye_mask(n), 1.0, 0.0).astype(jnp.float32)
    state = []
    for a in mats:
        top = jnp.max(jnp.sum(jnp.abs(a), axis=0, keepdims=True), axis=1, keepdims=True)
        top = jnp.maximum(top, 1.5)
        scale = 2.0 / (1.0 + top)
        err = (top - 1.0) / (top + 1.0)
        gain = 2.0 / (2.0 - err * err)
        r = eye - scale * a
        x = (gain * scale) * (eye + r)
        rs = split(r)
        r = (1.0 - gain) * eye + gain * mm3(rs, rs)
        state.append((x, r, err * err * gain * 0.5))
    between()
    for step in range(JOINT_STEPS + 1):
        later = []
        for x, r, err in state:
            gain = 2.0 / (2.0 - err * err)
            rs = split(r)
            x = gain * (x + joined(split(x), (rs[0], rs[0]), NN))
            if step < JOINT_STEPS:
                r = (1.0 - gain) * eye + gain * mm3(rs, rs)
            later.append((x, r, err * err * gain * 0.5))
        state = later
        between()
    exact = [eye - mm6(a, s[0]) for a, s in zip(mats, state)]
    between()
    mid = []
    for r, (x, _, _) in zip(exact, state):
        rs = split(r)
        mid.append((x + mm3(split(x), rs), mm3(rs, rs)))
    between()
    out = [x + mm3(split(x), split(r)) for x, r in mid]
    while others:
        between()
    return out


def place():
    xy, z, core = (lax.axis_index(a) for a in ("xy", "z", "core"))
    n_z, n_core = lax.axis_size("z"), lax.axis_size("core")
    return (xy * n_z + z) * n_core + core, xy * n_z + z, core


def onehots(picks_ref, device, rows):
    at = lax.broadcasted_iota(jnp.int32, (8, rows), 1)
    row = lax.broadcasted_iota(jnp.int32, (8, rows), 0)
    want = jnp.where(row == 0, picks_ref[0, device], jnp.where(row == 1, picks_ref[1, device], -1))
    return jnp.where(at == want, 1.0, 0.0)


def pick_kernel(picks_ref, frames_ref, out_ref):
    feats, rows = frames_ref.shape
    device, _, _ = place()
    chosen = mm(onehots(picks_ref, device, rows).astype(jnp.bfloat16), frames_ref[...], NT)
    same = jnp.where(picks_ref[0, device] == picks_ref[1, device], 1.0, 0.0)
    lane = lax.broadcasted_iota(jnp.int32, (1, LANES), 1)
    parts = []
    for s in range(2):
        for c in range(4):
            lo = c * LANES
            wide = min(LANES, feats - lo)
            piece = chosen[s : s + 1, lo : lo + wide]
            if wide < LANES:
                piece = jnp.concatenate([piece, jnp.zeros((1, LANES - wide), jnp.float32)], axis=1)
                piece = jnp.where(lane == wide, same, piece)
            parts.append(piece)
    row = jnp.concatenate(parts, axis=0).astype(jnp.bfloat16)
    out_ref[...] = jnp.broadcast_to(row[None], out_ref.shape)


def halves(ref, feats):
    width = ref.shape[1] // 2
    return [ref[:, s * width : s * width + feats] for s in range(2)]


def gauss(tall, flat, inner, feats):
    return jnp.exp(-(tall + flat - 2.0 * inner) * (0.5 / feats))


def diag_sums(inner, diag):
    masked = jnp.where(diag, inner, 0.0)
    return jnp.sum(masked, axis=1, keepdims=True), jnp.sum(masked, axis=0, keepdims=True)


def term_of(chosen, tall, frames, frame_sq, wsplit, feats):
    near = gauss(tall, frame_sq, mm(chosen, frames), feats)
    return mm3(wsplit, split(near), NT)


def frame_squares(frames):
    wide = frames.astype(jnp.float32)
    return jnp.sum(wide * wide, axis=0, keepdims=True)


def padded(ref, scratch):
    scratch[...] = jnp.zeros_like(scratch)
    scratch[: ref.shape[0], :] = ref[...].astype(jnp.float32)
    return scratch[...]


def own_kernel(
    picks_ref, own_ref, frames_ref, weights_ref, labels_ref, inv_ref, term_ref, tall_ref, flat_ref, w_scr, l_scr
):
    feats, rows = frames_ref.shape
    half = own_ref.shape[0]
    device, pos, _ = place()
    chosen = halves(own_ref, feats)
    diag = eye_mask(half)
    one = jnp.where(diag, RIDGE, 0.0)
    inner = [mm(c, c, NT) for c in chosen]
    sums = [diag_sums(g, diag) for g in inner]
    mats = [gauss(t, f, g, feats) + one for (t, f), g in zip(sums, inner)]
    for s in range(2):
        flat_ref[s : s + 1, :] = sums[s][1]
        tall_ref[:, s : s + 1] = sums[s][0]
    kept = {}

    def prepare():
        kept["frames"] = frames_ref[...]
        kept["squares"] = frame_squares(kept["frames"])
        weights = padded(weights_ref, w_scr)
        kept["weights"] = split(weights)
        kept["start"] = padded(labels_ref, l_scr) - RIDGE * weights
        kept["hot"] = onehots(picks_ref, device, rows)

    def term(s):
        def go():
            here = lax.broadcasted_iota(jnp.int32, (1, half), 1) == pos
            picked = jnp.sum(kept["start"] * kept["hot"][s : s + 1], axis=1, keepdims=True)
            summed = term_of(chosen[s], sums[s][0], kept["frames"], kept["squares"], kept["weights"], feats)
            term_ref[s] = jnp.where(here, picked, 0.0) - summed

        return go

    inv = inverses(mats, [prepare, term(0), term(1)])
    for s in range(2):
        inv_ref[s] = inv[s]


def rest_kernel(own_ref, other_ref, frames_ref, weights_ref, inv_ref, term_ref, tall_ref, flat_ref, out_ref, w_scr):
    feats, rows = frames_ref.shape
    half = own_ref.shape[0]
    width = own_ref.shape[1] // 2
    _, _, core = place()
    near = halves(own_ref, feats)
    far = halves(other_ref, feats)
    diag = eye_mask(half)
    one = jnp.where(diag, RIDGE, 0.0)
    inner = [mm(c, c, NT) for c in far]
    sums = [diag_sums(g, diag) for g in inner]
    talls = [[tall_ref[:, s : s + 1], sums[s][0]] for s in range(2)]
    flats = [[flat_ref[s : s + 1, :], sums[s][1]] for s in range(2)]
    chosen = [[near[s], far[s]] for s in range(2)]

    def block(s, i, t, j):
        return gauss(talls[s][i], flats[t][j], mm(chosen[s][i], chosen[t][j], NT), feats)

    inv = [inv_ref[s] for s in range(2)]
    upper = [block(s, 0, s, 1) for s in range(2)]
    lower, couple, schur = [], [], []
    for s in range(2):
        lower.append(block(s, 1, s, 0))
        couple.append(mm6_rows(inv[s], upper[s]))
    for s in range(2):
        corner = gauss(talls[s][1], flats[s][1], inner[s], feats) + one
        schur.append(corner - mm6_rows(lower[s], couple[s]))
    kept = {}

    def prepare():
        kept["frames"] = frames_ref[...]
        kept["squares"] = frame_squares(kept["frames"])
        kept["weights"] = split(padded(weights_ref, w_scr))

    def term(s):
        def go():
            kept["term", s] = -term_of(
                far[s], talls[s][1], kept["frames"], kept["squares"], kept["weights"], feats
            )

        return go

    def cross(i):
        def go():
            row = [block(1, i, 0, j) for j in range(2)]
            flag = (own_ref, other_ref)[i][:, width + feats : width + feats + 1].astype(jnp.float32)
            row[i] = row[i] + jnp.where(diag, RIDGE * flag, 0.0)
            kept["cross", i] = jnp.concatenate(row, axis=1)

        return go

    def forward(s, first, second):
        return mm6_rows(first, inv[s]), second - mm6_rows(first, couple[s])

    def early():
        kept["forward"] = forward(0, term_ref[0], kept["term", 0])

    last = inverses(schur, [prepare, term(0), early, term(1), cross(0), cross(1)])

    def backward(s, y, m):
        z = mm6_rows(m, last[s])
        return y - mm6_rows(z, couple[s], NT), z

    deltas = [backward(0, *kept["forward"])]
    both = jnp.concatenate(deltas[0], axis=1)
    first = term_ref[1] - mm6_rows(both, kept["cross", 0], NT)
    second = kept["term", 1] - mm6_rows(both, kept["cross", 1], NT)
    deltas.append(backward(1, *forward(1, first, second)))

    per = 16
    groups = half // per
    fill = jnp.zeros((2 * LANES - both.shape[0], half), jnp.float32)
    for i, slot in enumerate((core, 1 - core)):
        packed = None
        for s in range(2):
            full = jnp.concatenate([deltas[s][i], fill], axis=0)
            body = jnp.transpose(full[:LANES])
            out_ref[:, pl.ds(slot, 1), s * per : (s + 1) * per, :] = body.reshape(groups, 1, per, LANES)
            tail = jnp.transpose(full[LANES:]).reshape(groups, 2, 8, LANES)
            for g in range(2):
                piece = tail[:, g].reshape(groups * 8, LANES)
                turn = (2 * s + g) * 32
                if turn:
                    piece = pltpu.roll(piece, turn, 1)
                packed = piece if packed is None else packed + piece
        out_ref[:, pl.ds(slot, 1), 2 * per :, :] = packed.reshape(groups, 1, 8, LANES)


def mid_kernel(got_ref, out_ref):
    total = jnp.sum(got_ref[...], axis=0)
    per = 16
    rest = total[2 * per :]
    for s in range(2):
        out_ref[:, s, :] = total[s * per : (s + 1) * per]
        pieces = []
        for g in range(2):
            turn = (2 * s + g) * 32
            pieces.append(pltpu.roll(rest, LANES - turn, 1) if turn else rest)
        out_ref[:, 2 + s, :] = jnp.concatenate(pieces, axis=0)


def end_kernel(picks_ref, got_ref, weights_ref, out_ref):
    targets, rows = weights_ref.shape
    device, _, _ = place()
    total = jnp.sum(got_ref[...], axis=0)
    turned = jnp.transpose(jnp.concatenate([total, jnp.zeros((LANES - 4, LANES), jnp.float32)], axis=0))
    hot = onehots(picks_ref, device, rows)
    out_ref[:LANES, :] = weights_ref[:LANES, :] + (turned[:, 0:1] * hot[0:1] + turned[:, 1:2] * hot[1:2])
    left = targets - LANES
    out_ref[LANES:, :] = weights_ref[LANES:, :] + (
        turned[:left, 2:3] * hot[0:1] + turned[:left, 3:4] * hot[1:2]
    )


VMEM = pl.BlockSpec(memory_space=pltpu.VMEM)
SMEM = pl.BlockSpec(memory_space=pltpu.SMEM)


def kernel(body, ins, outs, scratch=(), flops=0):
    single = not isinstance(outs, list)
    return pl.pallas_call(
        body,
        in_specs=ins,
        out_specs=VMEM if single else [VMEM] * len(outs),
        out_shape=outs,
        scratch_shapes=list(scratch),
        compiler_params=pltpu.CompilerParams(vmem_limit_bytes=VMEM_BYTES),
        cost_estimate=pl.CostEstimate(flops=flops, bytes_accessed=1 << 20, transcendentals=0),
    )


def f32(*dims):
    return jax.ShapeDtypeStruct(dims, jnp.float32)


def update(got, other, frames, weights, labels, picks, n_xy):
    half = got.shape[0]
    targets, rows = weights.shape
    tall = -(-targets // 8) * 8
    scratch = pltpu.VMEM((tall, rows), jnp.float32)
    known = kernel(
        own_kernel,
        [SMEM] + [VMEM] * 4,
        [f32(2, half, half), f32(2, tall, half), f32(half, 2), f32(2, half)],
        [scratch, scratch],
        flops=6_000_000_000,
    )(picks, got, frames, weights, labels)
    return kernel(rest_kernel, [VMEM] * 8, f32(n_xy, 2, 40, LANES), [scratch], flops=6_000_000_000)(
        got, other, frames, weights, *known
    )


def shards(frames, labels, weights, picks):
    n_xy, n_z, n_core = (lax.axis_size(a) for a in ("xy", "z", "core"))
    frames, labels, weights = frames.T, labels.T, weights.T
    sent = pl.pallas_call(
        pick_kernel,
        grid=(1,),
        in_specs=[SMEM, pl.BlockSpec(frames.shape, lambda i: (0, 0))],
        out_specs=pl.BlockSpec((n_z, 8, LANES), lambda i: (0, 0, 0)),
        out_shape=jax.ShapeDtypeStruct((n_z, 8, LANES), jnp.bfloat16),
        compiler_params=pltpu.CompilerParams(vmem_limit_bytes=60 * 1024 * 1024),
    )(picks, frames)
    got = lax.all_to_all(sent, "z", 0, 0).reshape(n_z, 8 * LANES)
    got = lax.all_to_all(jnp.broadcast_to(got[None], (n_xy,) + got.shape), "xy", 0, 0)
    got = got.reshape(n_xy * n_z, 8 * LANES)
    other = lax.ppermute(got, "core", [(0, 1), (1, 0)])
    sent = update(got, other, frames, weights, labels, picks, n_xy)
    got = lax.all_to_all(sent.reshape(n_xy * n_core, 40, LANES), ("xy", "core"), 0, 0)
    part = kernel(mid_kernel, [VMEM], f32(n_z, 4, LANES))(got)
    got = lax.all_to_all(part, "z", 0, 0)
    return kernel(end_kernel, [SMEM, VMEM, VMEM], f32(*weights.shape))(picks, got, weights).T


def solution(mesh):
    grid = Mesh(mesh.devices.reshape(mesh.shape["row"], -1, 2), ("xy", "z", "core"))
    spread = P(("xy", "z", "core"), None)
    return jax.shard_map(
        shards, mesh=grid, in_specs=(spread, spread, spread, P()), out_specs=spread, check_vma=False
    )
```

```python
import jax
import jax.numpy as jnp
from jax import lax
from jax.experimental import pallas as pl
from jax.experimental.pallas import tpu as pltpu
from jax.sharding import Mesh, PartitionSpec as P

RIDGE = 1.0
LANES = 128
JOINT_STEPS = 4
VMEM_BYTES = 40 * 1024 * 1024

NN = (((1,), (0,)), ((), ()))
NT = (((1,), (1,)), ((), ()))


def mm(a, b, dims=NN):
    return lax.dot_general(a, b, dims, preferred_element_type=jnp.float32)


def split(a):
    hi = a.astype(jnp.bfloat16)
    lo = (a - hi.astype(jnp.float32)).astype(jnp.bfloat16)
    return hi, lo


def split3(a):
    hi = a.astype(jnp.bfloat16)
    rest = a - hi.astype(jnp.float32)
    mid = rest.astype(jnp.bfloat16)
    return hi, mid, (rest - mid.astype(jnp.float32)).astype(jnp.bfloat16)


def joined(left, right, dims):
    return mm(jnp.concatenate(left, axis=dims[0][0][0]), jnp.concatenate(right, axis=dims[0][1][0]), dims)


def mm3(a, b, dims=NN):
    return joined((a[0], a[1], a[0]), (b[0], b[0], b[1]), dims)


def split(a):
    hi = a.astype(jnp.bfloat16)
    lo = (a - hi.astype(jnp.float32)).astype(jnp.bfloat16)
    return hi, lo


def split3(a):
    hi = a.astype(jnp.bfloat16)
    rest = a - hi.astype(jnp.float32)
    mid = rest.astype(jnp.bfloat16)
    return hi, mid, (rest - mid.astype(jnp.float32)).astype(jnp.bfloat16)


def joined(left, right, dims):
    return mm(jnp.concatenate(left, axis=dims[0][0][0]), jnp.concatenate(right, axis=dims[0][1][0]), dims)


def mm3(a, b, dims=NN):
    return joined((a[0], a[1], a[0]), (b[0], b[0], b[1]), dims)


def mm6(a, b, dims=NN):
    a, b = split3(a), split3(b)
    return joined((a[0], a[1], a[2], a[0], a[1], a[0]), (b[0], b[0], b[0], b[1], b[1], b[2]), dims)


def mm6_rows(a, b, dims=NN):
    n = a.shape[0]
    a, b = split3(a), split3(b)
    p = mm(jnp.concatenate(a, axis=0), b[0], dims)
    q = mm(jnp.concatenate(a[:2], axis=0), b[1], dims)
    return p[:n] + (p[n : 2 * n] + q[:n]) + (p[2 * n :] + q[n:] + mm(a[0], b[2], dims))


def eye_mask(n):
    return lax.broadcasted_iota(jnp.int32, (n, n), 0) == lax.broadcasted_iota(jnp.int32, (n, n), 1)


def inverses(mats, others=()):
    others = list(others)

    def between():
        if others:
            others.pop(0)()

    n = mats[0].shape[0]
    eye = jnp.where(eye_mask(n), 1.0, 0.0).astype(jnp.float32)
    state = []
    for a in mats:
        top = jnp.max(jnp.sum(jnp.abs(a), axis=0, keepdims=True), axis=1, keepdims=True)
        top = jnp.maximum(top, 1.5)
        scale = 2.0 / (1.0 + top)
        err = (top - 1.0) / (top + 1.0)
        gain = 2.0 / (2.0 - err * err)
        r = eye - scale * a
        x = (gain * scale) * (eye + r)
        rs = split(r)
        r = (1.0 - gain) * eye + gain * mm3(rs, rs)
        state.append((x, r, err * err * gain * 0.5))
    between()
    for step in range(JOINT_STEPS + 1):
        later = []
        for x, r, err in state:
            gain = 2.0 / (2.0 - err * err)
            rs = split(r)
            x = gain * (x + joined(split(x), (rs[0], rs[0]), NN))
            if step < JOINT_STEPS:
                r = (1.0 - gain) * eye + gain * mm3(rs, rs)
            later.append((x, r, err * err * gain * 0.5))
        state = later
        between()
    exact = [eye - mm6(a, s[0]) for a, s in zip(mats, state)]
    between()
    mid = []
    for r, (x, _, _) in zip(exact, state):
        rs = split(r)
        mid.append((x + mm3(split(x), rs), mm3(rs, rs)))
    between()
    out = [x + mm3(split(x), split(r)) for x, r in mid]
    while others:
        between()
    return out


def place():
    xy, z, core = (lax.axis_index(a) for a in ("xy", "z", "core"))
    n_z, n_core = lax.axis_size("z"), lax.axis_size("core")
    return (xy * n_z + z) * n_core + core, xy * n_z + z, core


def onehots(picks_ref, device, rows):
    lane = lax.broadcasted_iota(jnp.int32, picks_ref.shape, 1)
    own = jnp.where(lane == device, picks_ref[...].astype(jnp.float32), 0.0)
    own = jnp.sum(own, axis=1, keepdims=True).astype(jnp.int32)
    return jnp.where(lax.broadcasted_iota(jnp.int32, (2, rows), 1) == own, 1.0, 0.0)


def pick_kernel(picks_ref, frames_ref, out_ref):
    feats, rows = frames_ref.shape
    device, _, _ = place()
    hot = onehots(picks_ref, device, rows)
    chosen = mm(hot.astype(jnp.bfloat16), frames_ref[...], NT)
    same = jnp.sum(hot[0:1] * hot[1:2], axis=1, keepdims=True)
    lane = lax.broadcasted_iota(jnp.int32, (1, LANES), 1)
    parts = []
    for s in range(2):
        for c in range(4):
            lo = c * LANES
            wide = min(LANES, feats - lo)
            piece = chosen[s : s + 1, lo : lo + wide]
            if wide < LANES:
                piece = jnp.concatenate([piece, jnp.zeros((1, LANES - wide), jnp.float32)], axis=1)
                piece = jnp.where(lane == wide, same, piece)
            parts.append(piece)
    row = jnp.concatenate(parts, axis=0).astype(jnp.bfloat16)
    out_ref[...] = jnp.broadcast_to(row[None], out_ref.shape)


def halves(ref, feats):
    width = ref.shape[1] // 2
    return [ref[:, s * width : s * width + feats] for s in range(2)]


def gauss(tall, flat, inner, feats):
    return jnp.exp(-(tall + flat - 2.0 * inner) * (0.5 / feats))


def diag_sums(inner, diag):
    masked = jnp.where(diag, inner, 0.0)
    return jnp.sum(masked, axis=1, keepdims=True), jnp.sum(masked, axis=0, keepdims=True)


def term_of(chosen, tall, frames, frame_sq, wsplit, feats):
    near = gauss(tall, frame_sq, mm(chosen, frames), feats)
    return mm3(wsplit, split(near), NT)


def frame_squares(frames):
    wide = frames.astype(jnp.float32)
    return jnp.sum(wide * wide, axis=0, keepdims=True)


def padded(ref, scratch):
    scratch[...] = jnp.zeros_like(scratch)
    scratch[: ref.shape[0], :] = ref[...].astype(jnp.float32)
    return scratch[...]


def own_kernel(
    picks_ref, own_ref, frames_ref, weights_ref, labels_ref, inv_ref, term_ref, tall_ref, flat_ref, w_scr, l_scr
):
    feats, rows = frames_ref.shape
    half = own_ref.shape[0]
    device, pos, _ = place()
    chosen = halves(own_ref, feats)
    diag = eye_mask(half)
    one = jnp.where(diag, RIDGE, 0.0)
    inner = [mm(c, c, NT) for c in chosen]
    sums = [diag_sums(g, diag) for g in inner]
    mats = [gauss(t, f, g, feats) + one for (t, f), g in zip(sums, inner)]
    for s in range(2):
        flat_ref[s : s + 1, :] = sums[s][1]
        tall_ref[:, s : s + 1] = sums[s][0]
    kept = {}

    def prepare():
        kept["frames"] = frames_ref[...]
        kept["squares"] = frame_squares(kept["frames"])
        weights = padded(weights_ref, w_scr)
        kept["weights"] = split(weights)
        kept["start"] = padded(labels_ref, l_scr) - RIDGE * weights
        kept["hot"] = onehots(picks_ref, device, rows)

    def term(s):
        def go():
            here = lax.broadcasted_iota(jnp.int32, (1, half), 1) == pos
            picked = jnp.sum(kept["start"] * kept["hot"][s : s + 1], axis=1, keepdims=True)
            summed = term_of(chosen[s], sums[s][0], kept["frames"], kept["squares"], kept["weights"], feats)
            term_ref[s] = jnp.where(here, picked, 0.0) - summed

        return go

    inv = inverses(mats, [prepare, term(0), term(1)])
    for s in range(2):
        inv_ref[s] = inv[s]


def rest_kernel(own_ref, other_ref, frames_ref, weights_ref, inv_ref, term_ref, tall_ref, flat_ref, out_ref, w_scr):
    feats, rows = frames_ref.shape
    half = own_ref.shape[0]
    width = own_ref.shape[1] // 2
    _, _, core = place()
    near = halves(own_ref, feats)
    far = halves(other_ref, feats)
    diag = eye_mask(half)
    one = jnp.where(diag, RIDGE, 0.0)
    inner = [mm(c, c, NT) for c in far]
    sums = [diag_sums(g, diag) for g in inner]
    talls = [[tall_ref[:, s : s + 1], sums[s][0]] for s in range(2)]
    flats = [[flat_ref[s : s + 1, :], sums[s][1]] for s in range(2)]
    chosen = [[near[s], far[s]] for s in range(2)]

    def block(s, i, t, j):
        return gauss(talls[s][i], flats[t][j], mm(chosen[s][i], chosen[t][j], NT), feats)

    inv = [inv_ref[s] for s in range(2)]
    upper = [block(s, 0, s, 1) for s in range(2)]
    lower, couple, schur = [], [], []
    for s in range(2):
        lower.append(block(s, 1, s, 0))
        couple.append(mm6_rows(inv[s], upper[s]))
    for s in range(2):
        corner = gauss(talls[s][1], flats[s][1], inner[s], feats) + one
        schur.append(corner - mm6_rows(lower[s], couple[s]))
    kept = {}

    def prepare():
        kept["frames"] = frames_ref[...]
        kept["squares"] = frame_squares(kept["frames"])
        kept["weights"] = split(padded(weights_ref, w_scr))

    def term(s):
        def go():
            kept["term", s] = -term_of(
                far[s], talls[s][1], kept["frames"], kept["squares"], kept["weights"], feats
            )

        return go

    def cross(i):
        def go():
            row = [block(1, i, 0, j) for j in range(2)]
            flag = (own_ref, other_ref)[i][:, width + feats : width + feats + 1].astype(jnp.float32)
            row[i] = row[i] + jnp.where(diag, RIDGE * flag, 0.0)
            kept["cross", i] = jnp.concatenate(row, axis=1)

        return go

    def forward(s, first, second):
        return mm6_rows(first, inv[s]), second - mm6_rows(first, couple[s])

    def early():
        kept["forward"] = forward(0, term_ref[0], kept["term", 0])

    last = inverses(schur, [prepare, term(0), early, term(1), cross(0), cross(1)])

    def backward(s, y, m):
        z = mm6_rows(m, last[s])
        return y - mm6_rows(z, couple[s], NT), z

    deltas = [backward(0, *kept["forward"])]
    both = jnp.concatenate(deltas[0], axis=1)
    first = term_ref[1] - mm6_rows(both, kept["cross", 0], NT)
    second = kept["term", 1] - mm6_rows(both, kept["cross", 1], NT)
    deltas.append(backward(1, *forward(1, first, second)))

    per = 16
    groups = half // per
    fill = jnp.zeros((2 * LANES - both.shape[0], half), jnp.float32)
    for i, slot in enumerate((core, 1 - core)):
        packed = None
        for s in range(2):
            full = jnp.concatenate([deltas[s][i], fill], axis=0)
            body = jnp.transpose(full[:LANES])
            out_ref[:, pl.ds(slot, 1), s * per : (s + 1) * per, :] = body.reshape(groups, 1, per, LANES)
            tail = jnp.transpose(full[LANES:]).reshape(groups, 2, 8, LANES)
            for g in range(2):
                piece = tail[:, g].reshape(groups * 8, LANES)
                turn = (2 * s + g) * 32
                if turn:
                    piece = pltpu.roll(piece, turn, 1)
                packed = piece if packed is None else packed + piece
        out_ref[:, pl.ds(slot, 1), 2 * per :, :] = packed.reshape(groups, 1, 8, LANES)


def mid_kernel(got_ref, out_ref):
    total = jnp.sum(got_ref[...], axis=0)
    per = 16
    rest = total[2 * per :]
    for s in range(2):
        out_ref[:, s, :] = total[s * per : (s + 1) * per]
        pieces = []
        for g in range(2):
            turn = (2 * s + g) * 32
            pieces.append(pltpu.roll(rest, LANES - turn, 1) if turn else rest)
        out_ref[:, 2 + s, :] = jnp.concatenate(pieces, axis=0)


def end_kernel(picks_ref, got_ref, weights_ref, out_ref):
    targets, rows = weights_ref.shape
    device, _, _ = place()
    total = jnp.sum(got_ref[...], axis=0)
    turned = jnp.transpose(jnp.concatenate([total, jnp.zeros((LANES - 4, LANES), jnp.float32)], axis=0))
    hot = onehots(picks_ref, device, rows)
    out_ref[:LANES, :] = weights_ref[:LANES, :] + (turned[:, 0:1] * hot[0:1] + turned[:, 1:2] * hot[1:2])
    left = targets - LANES
    out_ref[LANES:, :] = weights_ref[LANES:, :] + (
        turned[:left, 2:3] * hot[0:1] + turned[:left, 3:4] * hot[1:2]
    )


VMEM = pl.BlockSpec(memory_space=pltpu.VMEM)


def kernel(body, ins, outs, scratch=(), flops=0):
    single = not isinstance(outs, list)
    return pl.pallas_call(
        body,
        in_specs=ins,
        out_specs=VMEM if single else [VMEM] * len(outs),
        out_shape=outs,
        scratch_shapes=list(scratch),
        compiler_params=pltpu.CompilerParams(vmem_limit_bytes=VMEM_BYTES),
        cost_estimate=pl.CostEstimate(flops=flops, bytes_accessed=1 << 20, transcendentals=0),
    )


def f32(*dims):
    return jax.ShapeDtypeStruct(dims, jnp.float32)


def update(got, other, frames, weights, labels, picks, n_xy):
    half = got.shape[0]
    targets, rows = weights.shape
    tall = -(-targets // 8) * 8
    scratch = pltpu.VMEM((tall, rows), jnp.float32)
    known = kernel(
        own_kernel,
        [VMEM] * 5,
        [f32(2, half, half), f32(2, tall, half), f32(half, 2), f32(2, half)],
        [scratch, scratch],
        flops=6_000_000_000,
    )(picks, got, frames, weights, labels)
    return kernel(rest_kernel, [VMEM] * 8, f32(n_xy, 2, 40, LANES), [scratch], flops=6_000_000_000)(
        got, other, frames, weights, *known
    )


def shards(frames, labels, weights, picks):
    n_xy, n_z, n_core = (lax.axis_size(a) for a in ("xy", "z", "core"))
    frames, labels, weights = frames.T, labels.T, weights.T
    sent = pl.pallas_call(
        pick_kernel,
        grid=(1,),
        in_specs=[pl.BlockSpec(picks.shape, lambda i: (0, 0)), pl.BlockSpec(frames.shape, lambda i: (0, 0))],
        out_specs=pl.BlockSpec((n_z, 8, LANES), lambda i: (0, 0, 0)),
        out_shape=jax.ShapeDtypeStruct((n_z, 8, LANES), jnp.bfloat16),
        compiler_params=pltpu.CompilerParams(vmem_limit_bytes=60 * 1024 * 1024),
    )(picks, frames)
    got = lax.all_to_all(sent, "z", 0, 0).reshape(n_z, 8 * LANES)
    got = lax.all_to_all(jnp.broadcast_to(got[None], (n_xy,) + got.shape), "xy", 0, 0)
    got = got.reshape(n_xy * n_z, 8 * LANES)
    other = lax.ppermute(got, "core", [(0, 1), (1, 0)])
    sent = update(got, other, frames, weights, labels, picks, n_xy)
    got = lax.all_to_all(sent.reshape(n_xy * n_core, 40, LANES), ("xy", "core"), 0, 0)
    part = kernel(mid_kernel, [VMEM], f32(n_z, 4, LANES))(got)
    got = lax.all_to_all(part, "z", 0, 0)
    return kernel(end_kernel, [VMEM] * 3, f32(*weights.shape))(picks, got, weights).T


def solution(mesh):
    grid = Mesh(mesh.devices.reshape(mesh.shape["row"], -1, 2), ("xy", "z", "core"))
    spread = P(("xy", "z", "core"), None)
    return jax.shard_map(
        shards, mesh=grid, in_specs=(spread, spread, spread, P()), out_specs=spread, check_vma=False
    )
```

```python
import jax
import jax.numpy as jnp
from jax import lax
from jax.experimental import pallas as pl
from jax.experimental.pallas import tpu as pltpu
from jax.sharding import Mesh, PartitionSpec as P

RIDGE = 1.0
LANES = 128
JOINT_STEPS = 4
VMEM_BYTES = 40 * 1024 * 1024

NN = (((1,), (0,)), ((), ()))
NT = (((1,), (1,)), ((), ()))


def mm(a, b, dims=NN):
    return lax.dot_general(a, b, dims, preferred_element_type=jnp.float32)


def split(a):
    hi = a.astype(jnp.bfloat16)
    lo = (a - hi.astype(jnp.float32)).astype(jnp.bfloat16)
    return hi, lo


def split3(a):
    hi = a.astype(jnp.bfloat16)
    rest = a - hi.astype(jnp.float32)
    mid = rest.astype(jnp.bfloat16)
    return hi, mid, (rest - mid.astype(jnp.float32)).astype(jnp.bfloat16)


def joined(left, right, dims):
    return mm(jnp.concatenate(left, axis=dims[0][0][0]), jnp.concatenate(right, axis=dims[0][1][0]), dims)


def mm3(a, b, dims=NN):
    return joined((a[0], a[1], a[0]), (b[0], b[0], b[1]), dims)


def split(a):
    hi = a.astype(jnp.bfloat16)
    lo = (a - hi.astype(jnp.float32)).astype(jnp.bfloat16)
    return hi, lo


def split3(a):
    hi = a.astype(jnp.bfloat16)
    rest = a - hi.astype(jnp.float32)
    mid = rest.astype(jnp.bfloat16)
    return hi, mid, (rest - mid.astype(jnp.float32)).astype(jnp.bfloat16)


def joined(left, right, dims):
    return mm(jnp.concatenate(left, axis=dims[0][0][0]), jnp.concatenate(right, axis=dims[0][1][0]), dims)


def mm3(a, b, dims=NN):
    return joined((a[0], a[1], a[0]), (b[0], b[0], b[1]), dims)


def mm6(a, b, dims=NN):
    a, b = split3(a), split3(b)
    return joined((a[0], a[1], a[2], a[0], a[1], a[0]), (b[0], b[0], b[0], b[1], b[1], b[2]), dims)


def mm6_rows(a, b, dims=NN):
    n = a.shape[0]
    a, b = split3(a), split3(b)
    p = mm(jnp.concatenate(a, axis=0), b[0], dims)
    q = mm(jnp.concatenate(a[:2], axis=0), b[1], dims)
    return p[:n] + (p[n : 2 * n] + q[:n]) + (p[2 * n :] + q[n:] + mm(a[0], b[2], dims))


def eye_mask(n):
    return lax.broadcasted_iota(jnp.int32, (n, n), 0) == lax.broadcasted_iota(jnp.int32, (n, n), 1)


def inverses(mats, others=()):
    others = list(others)

    def between():
        if others:
            others.pop(0)()

    n = mats[0].shape[0]
    eye = jnp.where(eye_mask(n), 1.0, 0.0).astype(jnp.float32)
    state = []
    for a in mats:
        top = jnp.max(jnp.sum(jnp.abs(a), axis=0, keepdims=True), axis=1, keepdims=True)
        top = jnp.maximum(top, 1.5)
        scale = 2.0 / (1.0 + top)
        err = (top - 1.0) / (top + 1.0)
        gain = 2.0 / (2.0 - err * err)
        r = eye - scale * a
        x = (gain * scale) * (eye + r)
        rs = split(r)
        r = (1.0 - gain) * eye + gain * mm3(rs, rs)
        state.append((x, r, err * err * gain * 0.5))
    between()
    for step in range(JOINT_STEPS + 1):
        later = []
        for x, r, err in state:
            gain = 2.0 / (2.0 - err * err)
            rs = split(r)
            x = gain * (x + joined(split(x), (rs[0], rs[0]), NN))
            if step < JOINT_STEPS:
                r = (1.0 - gain) * eye + gain * mm3(rs, rs)
            later.append((x, r, err * err * gain * 0.5))
        state = later
        between()
    exact = [eye - mm6(a, s[0]) for a, s in zip(mats, state)]
    between()
    mid = []
    for r, (x, _, _) in zip(exact, state):
        rs = split(r)
        mid.append((x + mm3(split(x), rs), mm3(rs, rs)))
    between()
    out = [x + mm3(split(x), split(r)) for x, r in mid]
    while others:
        between()
    return out


def place():
    xy, z, core = (lax.axis_index(a) for a in ("xy", "z", "core"))
    n_z, n_core = lax.axis_size("z"), lax.axis_size("core")
    return (xy * n_z + z) * n_core + core, xy * n_z + z, core


def onehots(picks_ref, device, rows):
    lane = lax.broadcasted_iota(jnp.int32, picks_ref.shape, 1)
    own = jnp.where(lane == device, picks_ref[...].astype(jnp.float32), 0.0)
    own = jnp.sum(own, axis=1, keepdims=True).astype(jnp.int32)
    return jnp.where(lax.broadcasted_iota(jnp.int32, (2, rows), 1) == own, 1.0, 0.0)


def pick_kernel(picks_ref, frames_ref, out_ref):
    feats, rows = frames_ref.shape
    device, _, _ = place()
    hot = onehots(picks_ref, device, rows)
    chosen = mm(hot.astype(jnp.bfloat16), frames_ref[...], NT)
    same = jnp.sum(hot[0:1] * hot[1:2], axis=1, keepdims=True)
    lane = lax.broadcasted_iota(jnp.int32, (1, LANES), 1)
    parts = []
    for s in range(2):
        for c in range(4):
            lo = c * LANES
            wide = min(LANES, feats - lo)
            piece = chosen[s : s + 1, lo : lo + wide]
            if wide < LANES:
                piece = jnp.concatenate([piece, jnp.zeros((1, LANES - wide), jnp.float32)], axis=1)
                piece = jnp.where(lane == wide, same, piece)
            parts.append(piece)
    row = jnp.concatenate(parts, axis=0).astype(jnp.bfloat16)
    out_ref[...] = jnp.broadcast_to(row[None], out_ref.shape)


def halves(ref, feats):
    width = ref.shape[1] // 2
    return [ref[:, s * width : s * width + feats] for s in range(2)]


def gauss(tall, flat, inner, feats):
    return jnp.exp(-(tall + flat - 2.0 * inner) * (0.5 / feats))


def diag_sums(inner, diag):
    masked = jnp.where(diag, inner, 0.0)
    return jnp.sum(masked, axis=1, keepdims=True), jnp.sum(masked, axis=0, keepdims=True)


def term_of(chosen, tall, frames, frame_sq, wsplit, feats):
    near = gauss(tall, frame_sq, mm(chosen, frames), feats)
    return mm3(wsplit, split(near), NT)


def frame_squares(frames):
    wide = frames.astype(jnp.float32)
    return jnp.sum(wide * wide, axis=0, keepdims=True)


def padded(ref, scratch):
    scratch[...] = jnp.zeros_like(scratch)
    scratch[: ref.shape[0], :] = ref[...].astype(jnp.float32)
    return scratch[...]


def own_kernel(
    picks_ref, own_ref, frames_ref, weights_ref, labels_ref, inv_ref, term_ref, tall_ref, flat_ref, w_scr, l_scr
):
    feats, rows = frames_ref.shape
    half = own_ref.shape[0]
    device, pos, _ = place()
    chosen = halves(own_ref, feats)
    diag = eye_mask(half)
    one = jnp.where(diag, RIDGE, 0.0)
    inner = [mm(c, c, NT) for c in chosen]
    sums = [diag_sums(g, diag) for g in inner]
    mats = [gauss(t, f, g, feats) + one for (t, f), g in zip(sums, inner)]
    for s in range(2):
        flat_ref[s : s + 1, :] = sums[s][1]
        tall_ref[:, s : s + 1] = sums[s][0]
    kept = {}

    def prepare():
        kept["frames"] = frames_ref[...]
        kept["squares"] = frame_squares(kept["frames"])
        weights = padded(weights_ref, w_scr)
        kept["weights"] = split(weights)
        kept["start"] = padded(labels_ref, l_scr) - RIDGE * weights
        kept["hot"] = onehots(picks_ref, device, rows)

    def term(s):
        def go():
            here = lax.broadcasted_iota(jnp.int32, (1, half), 1) == pos
            picked = jnp.sum(kept["start"] * kept["hot"][s : s + 1], axis=1, keepdims=True)
            summed = term_of(chosen[s], sums[s][0], kept["frames"], kept["squares"], kept["weights"], feats)
            term_ref[s] = jnp.where(here, picked, 0.0) - summed

        return go

    inv = inverses(mats, [prepare, term(0), term(1)])
    for s in range(2):
        inv_ref[s] = inv[s]


def rest_kernel(
    own_ref, other_ref, frames_ref, weights_ref, inv_ref, term_ref, tall_ref, flat_ref, keep_ref, send_ref, w_scr
):
    feats, rows = frames_ref.shape
    half = own_ref.shape[0]
    width = own_ref.shape[1] // 2
    near = halves(own_ref, feats)
    far = halves(other_ref, feats)
    diag = eye_mask(half)
    one = jnp.where(diag, RIDGE, 0.0)
    inner = [mm(c, c, NT) for c in far]
    sums = [diag_sums(g, diag) for g in inner]
    talls = [[tall_ref[:, s : s + 1], sums[s][0]] for s in range(2)]
    flats = [[flat_ref[s : s + 1, :], sums[s][1]] for s in range(2)]
    chosen = [[near[s], far[s]] for s in range(2)]

    def block(s, i, t, j):
        return gauss(talls[s][i], flats[t][j], mm(chosen[s][i], chosen[t][j], NT), feats)

    inv = [inv_ref[s] for s in range(2)]
    upper = [block(s, 0, s, 1) for s in range(2)]
    lower, couple, schur = [], [], []
    for s in range(2):
        lower.append(block(s, 1, s, 0))
        couple.append(mm6_rows(inv[s], upper[s]))
    for s in range(2):
        corner = gauss(talls[s][1], flats[s][1], inner[s], feats) + one
        schur.append(corner - mm6_rows(lower[s], couple[s]))
    kept = {}

    def prepare():
        kept["frames"] = frames_ref[...]
        kept["squares"] = frame_squares(kept["frames"])
        kept["weights"] = split(padded(weights_ref, w_scr))

    def term(s):
        def go():
            kept["term", s] = -term_of(
                far[s], talls[s][1], kept["frames"], kept["squares"], kept["weights"], feats
            )

        return go

    def cross(i):
        def go():
            row = [block(1, i, 0, j) for j in range(2)]
            flag = (own_ref, other_ref)[i][:, width + feats : width + feats + 1].astype(jnp.float32)
            row[i] = row[i] + jnp.where(diag, RIDGE * flag, 0.0)
            kept["cross", i] = jnp.concatenate(row, axis=1)

        return go

    def forward(s, first, second):
        return mm6_rows(first, inv[s]), second - mm6_rows(first, couple[s])

    def early():
        kept["forward"] = forward(0, term_ref[0], kept["term", 0])

    last = inverses(schur, [prepare, term(0), early, term(1), cross(0), cross(1)])

    def backward(s, y, m):
        z = mm6_rows(m, last[s])
        return y - mm6_rows(z, couple[s], NT), z

    deltas = [backward(0, *kept["forward"])]
    both = jnp.concatenate(deltas[0], axis=1)
    first = term_ref[1] - mm6_rows(both, kept["cross", 0], NT)
    second = kept["term", 1] - mm6_rows(both, kept["cross", 1], NT)
    deltas.append(backward(1, *forward(1, first, second)))

    per = 16
    groups = half // per
    fill = jnp.zeros((2 * LANES - both.shape[0], half), jnp.float32)
    for i, out_ref in enumerate((keep_ref, send_ref)):
        packed = None
        for s in range(2):
            full = jnp.concatenate([deltas[s][i], fill], axis=0)
            out_ref[:, s * per : (s + 1) * per, :] = jnp.transpose(full[:LANES]).reshape(groups, per, LANES)
            tail = jnp.transpose(full[LANES:]).reshape(groups, 2, 8, LANES)
            for g in range(2):
                piece = tail[:, g].reshape(groups * 8, LANES)
                turn = (2 * s + g) * 32
                if turn:
                    piece = pltpu.roll(piece, turn, 1)
                packed = piece if packed is None else packed + piece
        out_ref[:, 2 * per :, :] = packed.reshape(groups, 8, LANES)


def mid_kernel(got_ref, out_ref):
    total = jnp.sum(got_ref[...], axis=0)
    per = 16
    rest = total[2 * per :]
    for s in range(2):
        out_ref[:, s, :] = total[s * per : (s + 1) * per]
        pieces = []
        for g in range(2):
            turn = (2 * s + g) * 32
            pieces.append(pltpu.roll(rest, LANES - turn, 1) if turn else rest)
        out_ref[:, 2 + s, :] = jnp.concatenate(pieces, axis=0)


def end_kernel(picks_ref, got_ref, weights_ref, out_ref):
    targets, rows = weights_ref.shape
    device, _, _ = place()
    total = jnp.sum(got_ref[...], axis=0)
    turned = jnp.transpose(jnp.concatenate([total, jnp.zeros((LANES - 4, LANES), jnp.float32)], axis=0))
    hot = onehots(picks_ref, device, rows)
    out_ref[:LANES, :] = weights_ref[:LANES, :] + (turned[:, 0:1] * hot[0:1] + turned[:, 1:2] * hot[1:2])
    left = targets - LANES
    out_ref[LANES:, :] = weights_ref[LANES:, :] + (
        turned[:left, 2:3] * hot[0:1] + turned[:left, 3:4] * hot[1:2]
    )


VMEM = pl.BlockSpec(memory_space=pltpu.VMEM)


def kernel(body, ins, outs, scratch=(), flops=0):
    single = not isinstance(outs, list)
    return pl.pallas_call(
        body,
        in_specs=ins,
        out_specs=VMEM if single else [VMEM] * len(outs),
        out_shape=outs,
        scratch_shapes=list(scratch),
        compiler_params=pltpu.CompilerParams(vmem_limit_bytes=VMEM_BYTES),
        cost_estimate=pl.CostEstimate(flops=flops, bytes_accessed=1 << 20, transcendentals=0),
    )


def f32(*dims):
    return jax.ShapeDtypeStruct(dims, jnp.float32)


def update(got, other, frames, weights, labels, picks, n_xy):
    half = got.shape[0]
    targets, rows = weights.shape
    tall = -(-targets // 8) * 8
    scratch = pltpu.VMEM((tall, rows), jnp.float32)
    known = kernel(
        own_kernel,
        [VMEM] * 5,
        [f32(2, half, half), f32(2, tall, half), f32(half, 2), f32(2, half)],
        [scratch, scratch],
        flops=6_000_000_000,
    )(picks, got, frames, weights, labels)
    return kernel(rest_kernel, [VMEM] * 8, [f32(n_xy, 40, LANES)] * 2, [scratch], flops=6_000_000_000)(
        got, other, frames, weights, *known
    )


def shards(frames, labels, weights, picks):
    n_xy, n_z = lax.axis_size("xy"), lax.axis_size("z")
    frames, labels, weights = frames.T, labels.T, weights.T
    sent = pl.pallas_call(
        pick_kernel,
        grid=(1,),
        in_specs=[pl.BlockSpec(picks.shape, lambda i: (0, 0)), pl.BlockSpec(frames.shape, lambda i: (0, 0))],
        out_specs=pl.BlockSpec((n_z, 8, LANES), lambda i: (0, 0, 0)),
        out_shape=jax.ShapeDtypeStruct((n_z, 8, LANES), jnp.bfloat16),
        compiler_params=pltpu.CompilerParams(vmem_limit_bytes=60 * 1024 * 1024),
    )(picks, frames)
    got = lax.all_to_all(sent, "z", 0, 0).reshape(n_z, 8 * LANES)
    got = lax.all_to_all(jnp.broadcast_to(got[None], (n_xy,) + got.shape), "xy", 0, 0)
    got = got.reshape(n_xy * n_z, 8 * LANES)
    other = lax.ppermute(got, "core", [(0, 1), (1, 0)])
    keep, send = update(got, other, frames, weights, labels, picks, n_xy)
    got = lax.all_to_all(keep + lax.ppermute(send, "core", [(0, 1), (1, 0)]), "xy", 0, 0)
    part = kernel(mid_kernel, [VMEM], f32(n_z, 4, LANES))(got)
    got = lax.all_to_all(part, "z", 0, 0)
    return kernel(end_kernel, [VMEM] * 3, f32(*weights.shape))(picks, got, weights).T


def solution(mesh):
    grid = Mesh(mesh.devices.reshape(mesh.shape["row"], -1, 2), ("xy", "z", "core"))
    spread = P(("xy", "z", "core"), None)
    return jax.shard_map(
        shards, mesh=grid, in_specs=(spread, spread, spread, P()), out_specs=spread, check_vma=False
    )
```

```python
import jax
import jax.numpy as jnp
from jax import lax
from jax.experimental import pallas as pl
from jax.experimental.pallas import tpu as pltpu
from jax.sharding import Mesh, PartitionSpec as P

RIDGE = 1.0
LANES = 128
JOINT_STEPS = 4
VMEM_BYTES = 40 * 1024 * 1024

NN = (((1,), (0,)), ((), ()))
NT = (((1,), (1,)), ((), ()))


def mm(a, b, dims=NN):
    return lax.dot_general(a, b, dims, preferred_element_type=jnp.float32)


def split(a):
    hi = a.astype(jnp.bfloat16)
    lo = (a - hi.astype(jnp.float32)).astype(jnp.bfloat16)
    return hi, lo


def split3(a):
    hi = a.astype(jnp.bfloat16)
    rest = a - hi.astype(jnp.float32)
    mid = rest.astype(jnp.bfloat16)
    return hi, mid, (rest - mid.astype(jnp.float32)).astype(jnp.bfloat16)


def joined(left, right, dims):
    return mm(jnp.concatenate(left, axis=dims[0][0][0]), jnp.concatenate(right, axis=dims[0][1][0]), dims)


def mm3(a, b, dims=NN):
    return joined((a[0], a[1], a[0]), (b[0], b[0], b[1]), dims)


def split(a):
    hi = a.astype(jnp.bfloat16)
    lo = (a - hi.astype(jnp.float32)).astype(jnp.bfloat16)
    return hi, lo


def split3(a):
    hi = a.astype(jnp.bfloat16)
    rest = a - hi.astype(jnp.float32)
    mid = rest.astype(jnp.bfloat16)
    return hi, mid, (rest - mid.astype(jnp.float32)).astype(jnp.bfloat16)


def joined(left, right, dims):
    return mm(jnp.concatenate(left, axis=dims[0][0][0]), jnp.concatenate(right, axis=dims[0][1][0]), dims)


def mm3(a, b, dims=NN):
    return joined((a[0], a[1], a[0]), (b[0], b[0], b[1]), dims)


def mm6(a, b, dims=NN):
    a, b = split3(a), split3(b)
    return joined((a[0], a[1], a[2], a[0], a[1], a[0]), (b[0], b[0], b[0], b[1], b[1], b[2]), dims)


def mm6_rows(a, b, dims=NN):
    n = a.shape[0]
    a, b = split3(a), split3(b)
    p = mm(jnp.concatenate(a, axis=0), b[0], dims)
    q = mm(jnp.concatenate(a[:2], axis=0), b[1], dims)
    return p[:n] + (p[n : 2 * n] + q[:n]) + (p[2 * n :] + q[n:] + mm(a[0], b[2], dims))


def eye_mask(n):
    return lax.broadcasted_iota(jnp.int32, (n, n), 0) == lax.broadcasted_iota(jnp.int32, (n, n), 1)


def inverses(mats, others=()):
    others = list(others)

    def between():
        if others:
            others.pop(0)()

    n = mats[0].shape[0]
    eye = jnp.where(eye_mask(n), 1.0, 0.0).astype(jnp.float32)
    state = []
    for a in mats:
        top = jnp.max(jnp.sum(jnp.abs(a), axis=0, keepdims=True), axis=1, keepdims=True)
        top = jnp.maximum(top, 1.5)
        scale = 2.0 / (1.0 + top)
        err = (top - 1.0) / (top + 1.0)
        gain = 2.0 / (2.0 - err * err)
        r = eye - scale * a
        x = (gain * scale) * (eye + r)
        rs = split(r)
        r = (1.0 - gain) * eye + gain * mm3(rs, rs)
        state.append((x, r, err * err * gain * 0.5))
    between()
    for step in range(JOINT_STEPS + 1):
        later = []
        for x, r, err in state:
            gain = 2.0 / (2.0 - err * err)
            rs = split(r)
            x = gain * (x + joined(split(x), (rs[0], rs[0]), NN))
            if step < JOINT_STEPS:
                r = (1.0 - gain) * eye + gain * mm3(rs, rs)
            later.append((x, r, err * err * gain * 0.5))
        state = later
        between()
    exact = [eye - mm6(a, s[0]) for a, s in zip(mats, state)]
    between()
    mid = []
    for r, (x, _, _) in zip(exact, state):
        rs = split(r)
        mid.append((x + mm3(split(x), rs), mm3(rs, rs)))
    between()
    out = [x + mm3(split(x), split(r)) for x, r in mid]
    while others:
        between()
    return out


def place():
    xy, z, core = (lax.axis_index(a) for a in ("xy", "z", "core"))
    n_z, n_core = lax.axis_size("z"), lax.axis_size("core")
    return (xy * n_z + z) * n_core + core, xy * n_z + z, core


def onehots(picks_ref, device, rows):
    lane = lax.broadcasted_iota(jnp.int32, picks_ref.shape, 1)
    own = jnp.where(lane == device, picks_ref[...].astype(jnp.float32), 0.0)
    own = jnp.sum(own, axis=1, keepdims=True).astype(jnp.int32)
    return jnp.where(lax.broadcasted_iota(jnp.int32, (2, rows), 1) == own, 1.0, 0.0)


def pick_kernel(picks_ref, frames_ref, out_ref):
    feats, rows = frames_ref.shape
    device, _, _ = place()
    hot = onehots(picks_ref, device, rows)
    chosen = mm(hot.astype(jnp.bfloat16), frames_ref[...], NT)
    same = jnp.sum(hot[0:1] * hot[1:2], axis=1, keepdims=True)
    lane = lax.broadcasted_iota(jnp.int32, (1, LANES), 1)
    parts = []
    for s in range(2):
        for c in range(4):
            lo = c * LANES
            wide = min(LANES, feats - lo)
            piece = chosen[s : s + 1, lo : lo + wide]
            if wide < LANES:
                piece = jnp.concatenate([piece, jnp.zeros((1, LANES - wide), jnp.float32)], axis=1)
                piece = jnp.where(lane == wide, same, piece)
            parts.append(piece)
    row = jnp.concatenate(parts, axis=0).astype(jnp.bfloat16)
    out_ref[...] = jnp.broadcast_to(row[None], out_ref.shape)


def halves(ref, feats):
    width = ref.shape[1] // 2
    return [ref[:, s * width : s * width + feats] for s in range(2)]


def gauss(tall, flat, inner, feats):
    return jnp.exp(-(tall + flat - 2.0 * inner) * (0.5 / feats))


def diag_sums(inner, diag):
    masked = jnp.where(diag, inner, 0.0)
    return jnp.sum(masked, axis=1, keepdims=True), jnp.sum(masked, axis=0, keepdims=True)


def term_of(chosen, tall, frames, frame_sq, wsplit, feats):
    near = gauss(tall, frame_sq, mm(chosen, frames), feats)
    return mm3(wsplit, split(near), NT)


def frame_squares(frames):
    wide = frames.astype(jnp.float32)
    return jnp.sum(wide * wide, axis=0, keepdims=True)


def padded(ref, scratch):
    scratch[...] = jnp.zeros_like(scratch)
    scratch[: ref.shape[0], :] = ref[...].astype(jnp.float32)
    return scratch[...]


def own_kernel(
    picks_ref, own_ref, frames_ref, weights_ref, labels_ref, inv_ref, term_ref, tall_ref, flat_ref, w_scr, l_scr
):
    feats, rows = frames_ref.shape
    half = own_ref.shape[0]
    device, pos, _ = place()
    chosen = halves(own_ref, feats)
    diag = eye_mask(half)
    one = jnp.where(diag, RIDGE, 0.0)
    inner = [mm(c, c, NT) for c in chosen]
    sums = [diag_sums(g, diag) for g in inner]
    mats = [gauss(t, f, g, feats) + one for (t, f), g in zip(sums, inner)]
    for s in range(2):
        flat_ref[s : s + 1, :] = sums[s][1]
        tall_ref[:, s : s + 1] = sums[s][0]
    kept = {}

    def prepare():
        kept["frames"] = frames_ref[...]
        kept["squares"] = frame_squares(kept["frames"])
        weights = padded(weights_ref, w_scr)
        kept["weights"] = split(weights)
        kept["start"] = padded(labels_ref, l_scr) - RIDGE * weights
        kept["hot"] = onehots(picks_ref, device, rows)

    def term(s):
        def go():
            here = lax.broadcasted_iota(jnp.int32, (1, half), 1) == pos
            picked = jnp.sum(kept["start"] * kept["hot"][s : s + 1], axis=1, keepdims=True)
            summed = term_of(chosen[s], sums[s][0], kept["frames"], kept["squares"], kept["weights"], feats)
            term_ref[s] = jnp.where(here, picked, 0.0) - summed

        return go

    inv = inverses(mats, [prepare, term(0), term(1)])
    for s in range(2):
        inv_ref[s] = inv[s]


def rest_kernel(
    own_ref, other_ref, frames_ref, weights_ref, inv_ref, term_ref, tall_ref, flat_ref, send_ref, part_ref, couple_ref, w_scr
):
    feats, rows = frames_ref.shape
    half = own_ref.shape[0]
    width = own_ref.shape[1] // 2
    near = halves(own_ref, feats)
    far = halves(other_ref, feats)
    diag = eye_mask(half)
    one = jnp.where(diag, RIDGE, 0.0)
    inner = [mm(c, c, NT) for c in far]
    sums = [diag_sums(g, diag) for g in inner]
    talls = [[tall_ref[:, s : s + 1], sums[s][0]] for s in range(2)]
    flats = [[flat_ref[s : s + 1, :], sums[s][1]] for s in range(2)]
    chosen = [[near[s], far[s]] for s in range(2)]

    def block(s, i, t, j):
        return gauss(talls[s][i], flats[t][j], mm(chosen[s][i], chosen[t][j], NT), feats)

    inv = [inv_ref[s] for s in range(2)]
    upper = [block(s, 0, s, 1) for s in range(2)]
    lower, couple, schur = [], [], []
    for s in range(2):
        lower.append(block(s, 1, s, 0))
        couple.append(mm6_rows(inv[s], upper[s]))
    for s in range(2):
        corner = gauss(talls[s][1], flats[s][1], inner[s], feats) + one
        schur.append(corner - mm6_rows(lower[s], couple[s]))
    kept = {}

    def prepare():
        kept["frames"] = frames_ref[...]
        kept["squares"] = frame_squares(kept["frames"])
        kept["weights"] = split(padded(weights_ref, w_scr))

    def term(s):
        def go():
            kept["term", s] = -term_of(
                far[s], talls[s][1], kept["frames"], kept["squares"], kept["weights"], feats
            )

        return go

    def cross(i):
        def go():
            row = [block(1, i, 0, j) for j in range(2)]
            flag = (own_ref, other_ref)[i][:, width + feats : width + feats + 1].astype(jnp.float32)
            row[i] = row[i] + jnp.where(diag, RIDGE * flag, 0.0)
            kept["cross", i] = jnp.concatenate(row, axis=1)

        return go

    def forward(s, first, second):
        return mm6_rows(first, inv[s]), second - mm6_rows(first, couple[s])

    def early():
        kept["forward"] = forward(0, term_ref[0], kept["term", 0])

    last = inverses(schur, [prepare, term(0), early, term(1), cross(0), cross(1)])

    y, m = kept["forward"]
    far0 = mm6_rows(m, last[0])
    own0 = y - mm6_rows(far0, couple[0], NT)
    both = jnp.concatenate([own0, far0], axis=1)
    first = term_ref[1] - mm6_rows(both, kept["cross", 0], NT)
    second = kept["term", 1] - mm6_rows(both, kept["cross", 1], NT)
    y, m = forward(1, first, second)
    far1 = mm6_rows(m, last[1])
    pack((far0, far1), send_ref)
    for i, part in enumerate((own0, y, far1)):
        part_ref[i] = part
    couple_ref[...] = couple[1]


def pack(deltas, out_ref):
    rows, half = deltas[0].shape
    per = 16
    groups = half // per
    fill = jnp.zeros((2 * LANES - rows, half), jnp.float32)
    packed = None
    for s in range(2):
        full = jnp.concatenate([deltas[s], fill], axis=0)
        out_ref[:, s * per : (s + 1) * per, :] = jnp.transpose(full[:LANES]).reshape(groups, per, LANES)
        tail = jnp.transpose(full[LANES:]).reshape(groups, 2, 8, LANES)
        for g in range(2):
            piece = tail[:, g].reshape(groups * 8, LANES)
            turn = (2 * s + g) * 32
            if turn:
                piece = pltpu.roll(piece, turn, 1)
            packed = piece if packed is None else packed + piece
    out_ref[:, 2 * per :, :] = packed.reshape(groups, 8, LANES)


def finish_kernel(part_ref, couple_ref, keep_ref):
    own1 = part_ref[1] - mm6_rows(part_ref[2], couple_ref[...], NT)
    pack((part_ref[0], own1), keep_ref)


def mid_kernel(got_ref, out_ref):
    total = jnp.sum(got_ref[...], axis=0)
    per = 16
    rest = total[2 * per :]
    for s in range(2):
        out_ref[:, s, :] = total[s * per : (s + 1) * per]
        pieces = []
        for g in range(2):
            turn = (2 * s + g) * 32
            pieces.append(pltpu.roll(rest, LANES - turn, 1) if turn else rest)
        out_ref[:, 2 + s, :] = jnp.concatenate(pieces, axis=0)


def end_kernel(picks_ref, got_ref, weights_ref, out_ref):
    targets, rows = weights_ref.shape
    device, _, _ = place()
    total = jnp.sum(got_ref[...], axis=0)
    turned = jnp.transpose(jnp.concatenate([total, jnp.zeros((LANES - 4, LANES), jnp.float32)], axis=0))
    hot = onehots(picks_ref, device, rows)
    out_ref[:LANES, :] = weights_ref[:LANES, :] + (turned[:, 0:1] * hot[0:1] + turned[:, 1:2] * hot[1:2])
    left = targets - LANES
    out_ref[LANES:, :] = weights_ref[LANES:, :] + (
        turned[:left, 2:3] * hot[0:1] + turned[:left, 3:4] * hot[1:2]
    )


VMEM = pl.BlockSpec(memory_space=pltpu.VMEM)


def kernel(body, ins, outs, scratch=(), flops=0):
    single = not isinstance(outs, list)
    return pl.pallas_call(
        body,
        in_specs=ins,
        out_specs=VMEM if single else [VMEM] * len(outs),
        out_shape=outs,
        scratch_shapes=list(scratch),
        compiler_params=pltpu.CompilerParams(vmem_limit_bytes=VMEM_BYTES),
        cost_estimate=pl.CostEstimate(flops=flops, bytes_accessed=1 << 20, transcendentals=0),
    )


def f32(*dims):
    return jax.ShapeDtypeStruct(dims, jnp.float32)


def update(got, other, frames, weights, labels, picks, n_xy):
    half = got.shape[0]
    targets, rows = weights.shape
    tall = -(-targets // 8) * 8
    scratch = pltpu.VMEM((tall, rows), jnp.float32)
    known = kernel(
        own_kernel,
        [VMEM] * 5,
        [f32(2, half, half), f32(2, tall, half), f32(half, 2), f32(2, half)],
        [scratch, scratch],
        flops=6_000_000_000,
    )(picks, got, frames, weights, labels)
    send, part, couple = kernel(
        rest_kernel,
        [VMEM] * 8,
        [f32(n_xy, 40, LANES), f32(3, tall, half), f32(half, half)],
        [scratch],
        flops=6_000_000_000,
    )(got, other, frames, weights, *known)
    keep = kernel(finish_kernel, [VMEM] * 2, f32(n_xy, 40, LANES), flops=500_000_000)(part, couple)
    return keep, send


def shards(frames, labels, weights, picks):
    n_xy, n_z = lax.axis_size("xy"), lax.axis_size("z")
    frames, labels, weights = frames.T, labels.T, weights.T
    sent = pl.pallas_call(
        pick_kernel,
        grid=(1,),
        in_specs=[pl.BlockSpec(picks.shape, lambda i: (0, 0)), pl.BlockSpec(frames.shape, lambda i: (0, 0))],
        out_specs=pl.BlockSpec((n_z, 8, LANES), lambda i: (0, 0, 0)),
        out_shape=jax.ShapeDtypeStruct((n_z, 8, LANES), jnp.bfloat16),
        compiler_params=pltpu.CompilerParams(vmem_limit_bytes=60 * 1024 * 1024),
    )(picks, frames)
    got = lax.all_to_all(sent, "z", 0, 0).reshape(n_z, 8 * LANES)
    got = lax.all_to_all(jnp.broadcast_to(got[None], (n_xy,) + got.shape), "xy", 0, 0)
    got = got.reshape(n_xy * n_z, 8 * LANES)
    other = lax.ppermute(got, "core", [(0, 1), (1, 0)])
    keep, send = update(got, other, frames, weights, labels, picks, n_xy)
    got = lax.all_to_all(keep + lax.ppermute(send, "core", [(0, 1), (1, 0)]), "xy", 0, 0)
    part = kernel(mid_kernel, [VMEM], f32(n_z, 4, LANES))(got)
    got = lax.all_to_all(part, "z", 0, 0)
    return kernel(end_kernel, [VMEM] * 3, f32(*weights.shape))(picks, got, weights).T


def solution(mesh):
    grid = Mesh(mesh.devices.reshape(mesh.shape["row"], -1, 2), ("xy", "z", "core"))
    spread = P(("xy", "z", "core"), None)
    return jax.shard_map(
        shards, mesh=grid, in_specs=(spread, spread, spread, P()), out_specs=spread, check_vma=False
    )
```

```python
import jax
import jax.numpy as jnp
from jax import lax
from jax.experimental import pallas as pl
from jax.experimental.pallas import tpu as pltpu
from jax.sharding import Mesh, PartitionSpec as P

RIDGE = 1.0
LANES = 128
JOINT_STEPS = 4
VMEM_BYTES = 40 * 1024 * 1024

NN = (((1,), (0,)), ((), ()))
NT = (((1,), (1,)), ((), ()))


def mm(a, b, dims=NN):
    return lax.dot_general(a, b, dims, preferred_element_type=jnp.float32)


def split(a):
    hi = a.astype(jnp.bfloat16)
    lo = (a - hi.astype(jnp.float32)).astype(jnp.bfloat16)
    return hi, lo


def split3(a):
    hi = a.astype(jnp.bfloat16)
    rest = a - hi.astype(jnp.float32)
    mid = rest.astype(jnp.bfloat16)
    return hi, mid, (rest - mid.astype(jnp.float32)).astype(jnp.bfloat16)


def joined(left, right, dims):
    return mm(jnp.concatenate(left, axis=dims[0][0][0]), jnp.concatenate(right, axis=dims[0][1][0]), dims)


def mm3(a, b, dims=NN):
    return joined((a[0], a[1], a[0]), (b[0], b[0], b[1]), dims)


def split(a):
    hi = a.astype(jnp.bfloat16)
    lo = (a - hi.astype(jnp.float32)).astype(jnp.bfloat16)
    return hi, lo


def split3(a):
    hi = a.astype(jnp.bfloat16)
    rest = a - hi.astype(jnp.float32)
    mid = rest.astype(jnp.bfloat16)
    return hi, mid, (rest - mid.astype(jnp.float32)).astype(jnp.bfloat16)


def joined(left, right, dims):
    return mm(jnp.concatenate(left, axis=dims[0][0][0]), jnp.concatenate(right, axis=dims[0][1][0]), dims)


def mm3(a, b, dims=NN):
    return joined((a[0], a[1], a[0]), (b[0], b[0], b[1]), dims)


def mm6(a, b, dims=NN):
    a, b = split3(a), split3(b)
    return joined((a[0], a[1], a[2], a[0], a[1], a[0]), (b[0], b[0], b[0], b[1], b[1], b[2]), dims)


def mm6_rows(a, b, dims=NN):
    n = a.shape[0]
    a, b = split3(a), split3(b)
    p = mm(jnp.concatenate(a, axis=0), b[0], dims)
    q = mm(jnp.concatenate(a[:2], axis=0), b[1], dims)
    return p[:n] + (p[n : 2 * n] + q[:n]) + (p[2 * n :] + q[n:] + mm(a[0], b[2], dims))


def eye_mask(n):
    return lax.broadcasted_iota(jnp.int32, (n, n), 0) == lax.broadcasted_iota(jnp.int32, (n, n), 1)


def inverses(mats, others=()):
    others = list(others)

    def between():
        if others:
            others.pop(0)()

    n = mats[0].shape[0]
    eye = jnp.where(eye_mask(n), 1.0, 0.0).astype(jnp.float32)
    state = []
    for a in mats:
        top = jnp.max(jnp.sum(jnp.abs(a), axis=0, keepdims=True), axis=1, keepdims=True)
        top = jnp.maximum(top, 1.5)
        scale = 2.0 / (1.0 + top)
        err = (top - 1.0) / (top + 1.0)
        gain = 2.0 / (2.0 - err * err)
        r = eye - scale * a
        x = (gain * scale) * (eye + r)
        rs = split(r)
        r = (1.0 - gain) * eye + gain * mm3(rs, rs)
        state.append((x, r, err * err * gain * 0.5))
    between()
    for step in range(JOINT_STEPS + 1):
        later = []
        for x, r, err in state:
            gain = 2.0 / (2.0 - err * err)
            rs = split(r)
            x = gain * (x + joined(split(x), (rs[0], rs[0]), NN))
            if step < JOINT_STEPS:
                r = (1.0 - gain) * eye + gain * mm3(rs, rs)
            later.append((x, r, err * err * gain * 0.5))
        state = later
        between()
    exact = [eye - mm6(s[0], a) for a, s in zip(mats, state)]
    between()
    mid = []
    for r, (x, _, _) in zip(exact, state):
        rs = split(r)
        mid.append((x + mm3(rs, split(x)), mm(rs[0], rs[0])))
    between()
    out = [x + joined((r.astype(jnp.bfloat16),) * 2, split(x), NN) for x, r in mid]
    while others:
        between()
    return out


def place():
    xy, z, core = (lax.axis_index(a) for a in ("xy", "z", "core"))
    n_z, n_core = lax.axis_size("z"), lax.axis_size("core")
    return (xy * n_z + z) * n_core + core, xy * n_z + z, core


def onehots(picks_ref, device, rows):
    lane = lax.broadcasted_iota(jnp.int32, picks_ref.shape, 1)
    own = jnp.where(lane == device, picks_ref[...].astype(jnp.float32), 0.0)
    own = jnp.sum(own, axis=1, keepdims=True).astype(jnp.int32)
    return jnp.where(lax.broadcasted_iota(jnp.int32, (2, rows), 1) == own, 1.0, 0.0)


def pick_kernel(picks_ref, frames_ref, out_ref):
    feats, rows = frames_ref.shape
    device, _, _ = place()
    hot = onehots(picks_ref, device, rows)
    chosen = mm(hot.astype(jnp.bfloat16), frames_ref[...], NT)
    same = jnp.sum(hot[0:1] * hot[1:2], axis=1, keepdims=True)
    lane = lax.broadcasted_iota(jnp.int32, (1, LANES), 1)
    parts = []
    for s in range(2):
        for c in range(4):
            lo = c * LANES
            wide = min(LANES, feats - lo)
            piece = chosen[s : s + 1, lo : lo + wide]
            if wide < LANES:
                piece = jnp.concatenate([piece, jnp.zeros((1, LANES - wide), jnp.float32)], axis=1)
                piece = jnp.where(lane == wide, same, piece)
            parts.append(piece)
    row = jnp.concatenate(parts, axis=0).astype(jnp.bfloat16)
    out_ref[...] = jnp.broadcast_to(row[None], out_ref.shape)


def halves(ref, feats):
    width = ref.shape[1] // 2
    return [ref[:, s * width : s * width + feats] for s in range(2)]


def gauss(tall, flat, inner, feats):
    return jnp.exp(-(tall + flat - 2.0 * inner) * (0.5 / feats))


def diag_sums(inner, diag):
    masked = jnp.where(diag, inner, 0.0)
    return jnp.sum(masked, axis=1, keepdims=True), jnp.sum(masked, axis=0, keepdims=True)


def term_of(chosen, tall, frames, frame_sq, wsplit, feats):
    near = gauss(tall, frame_sq, mm(chosen, frames), feats)
    return mm3(wsplit, split(near), NT)


def frame_squares(frames):
    wide = frames.astype(jnp.float32)
    return jnp.sum(wide * wide, axis=0, keepdims=True)


def padded(ref, scratch):
    scratch[...] = jnp.zeros_like(scratch)
    scratch[: ref.shape[0], :] = ref[...].astype(jnp.float32)
    return scratch[...]


def own_kernel(
    picks_ref, own_ref, frames_ref, weights_ref, labels_ref, inv_ref, term_ref, tall_ref, flat_ref, w_scr, l_scr
):
    feats, rows = frames_ref.shape
    half = own_ref.shape[0]
    device, pos, _ = place()
    chosen = halves(own_ref, feats)
    diag = eye_mask(half)
    one = jnp.where(diag, RIDGE, 0.0)
    inner = [mm(c, c, NT) for c in chosen]
    sums = [diag_sums(g, diag) for g in inner]
    mats = [gauss(t, f, g, feats) + one for (t, f), g in zip(sums, inner)]
    for s in range(2):
        flat_ref[s : s + 1, :] = sums[s][1]
        tall_ref[:, s : s + 1] = sums[s][0]
    kept = {}

    def prepare():
        kept["frames"] = frames_ref[...]
        kept["squares"] = frame_squares(kept["frames"])
        weights = padded(weights_ref, w_scr)
        kept["weights"] = split(weights)
        kept["start"] = padded(labels_ref, l_scr) - RIDGE * weights
        kept["hot"] = onehots(picks_ref, device, rows)

    def term(s):
        def go():
            here = lax.broadcasted_iota(jnp.int32, (1, half), 1) == pos
            picked = jnp.sum(kept["start"] * kept["hot"][s : s + 1], axis=1, keepdims=True)
            summed = term_of(chosen[s], sums[s][0], kept["frames"], kept["squares"], kept["weights"], feats)
            term_ref[s] = jnp.where(here, picked, 0.0) - summed

        return go

    inv = inverses(mats, [prepare, term(0), term(1)])
    for s in range(2):
        inv_ref[s] = inv[s]


def rest_kernel(
    own_ref, other_ref, frames_ref, weights_ref, inv_ref, term_ref, tall_ref, flat_ref, send_ref, part_ref, couple_ref, w_scr
):
    feats, rows = frames_ref.shape
    half = own_ref.shape[0]
    width = own_ref.shape[1] // 2
    near = halves(own_ref, feats)
    far = halves(other_ref, feats)
    diag = eye_mask(half)
    one = jnp.where(diag, RIDGE, 0.0)
    inner = [mm(c, c, NT) for c in far]
    sums = [diag_sums(g, diag) for g in inner]
    talls = [[tall_ref[:, s : s + 1], sums[s][0]] for s in range(2)]
    flats = [[flat_ref[s : s + 1, :], sums[s][1]] for s in range(2)]
    chosen = [[near[s], far[s]] for s in range(2)]

    def block(s, i, t, j):
        return gauss(talls[s][i], flats[t][j], mm(chosen[s][i], chosen[t][j], NT), feats)

    inv = [inv_ref[s] for s in range(2)]
    upper = [block(s, 0, s, 1) for s in range(2)]
    lower, couple, schur = [], [], []
    for s in range(2):
        lower.append(block(s, 1, s, 0))
        couple.append(mm6_rows(inv[s], upper[s]))
    for s in range(2):
        corner = gauss(talls[s][1], flats[s][1], inner[s], feats) + one
        schur.append(corner - mm6_rows(lower[s], couple[s]))
    kept = {}

    def prepare():
        kept["frames"] = frames_ref[...]
        kept["squares"] = frame_squares(kept["frames"])
        kept["weights"] = split(padded(weights_ref, w_scr))

    def term(s):
        def go():
            kept["term", s] = -term_of(
                far[s], talls[s][1], kept["frames"], kept["squares"], kept["weights"], feats
            )

        return go

    def cross(i):
        def go():
            row = [block(1, i, 0, j) for j in range(2)]
            flag = (own_ref, other_ref)[i][:, width + feats : width + feats + 1].astype(jnp.float32)
            row[i] = row[i] + jnp.where(diag, RIDGE * flag, 0.0)
            kept["cross", i] = jnp.concatenate(row, axis=1)

        return go

    def forward(s, first, second):
        return mm6_rows(first, inv[s]), second - mm6_rows(first, couple[s])

    def early():
        kept["forward"] = forward(0, term_ref[0], kept["term", 0])

    last = inverses(schur, [prepare, term(0), early, term(1), cross(0), cross(1)])

    y, m = kept["forward"]
    far0 = mm6_rows(m, last[0])
    own0 = y - mm6_rows(far0, couple[0], NT)
    both = jnp.concatenate([own0, far0], axis=1)
    first = term_ref[1] - mm6_rows(both, kept["cross", 0], NT)
    second = kept["term", 1] - mm6_rows(both, kept["cross", 1], NT)
    y, m = forward(1, first, second)
    far1 = mm6_rows(m, last[1])
    pack((far0, far1), send_ref)
    for i, part in enumerate((own0, y, far1)):
        part_ref[i] = part
    couple_ref[...] = couple[1]


def pack(deltas, out_ref):
    rows, half = deltas[0].shape
    per = 16
    groups = half // per
    fill = jnp.zeros((2 * LANES - rows, half), jnp.float32)
    packed = None
    for s in range(2):
        full = jnp.concatenate([deltas[s], fill], axis=0)
        out_ref[:, s * per : (s + 1) * per, :] = jnp.transpose(full[:LANES]).reshape(groups, per, LANES)
        tail = jnp.transpose(full[LANES:]).reshape(groups, 2, 8, LANES)
        for g in range(2):
            piece = tail[:, g].reshape(groups * 8, LANES)
            turn = (2 * s + g) * 32
            if turn:
                piece = pltpu.roll(piece, turn, 1)
            packed = piece if packed is None else packed + piece
    out_ref[:, 2 * per :, :] = packed.reshape(groups, 8, LANES)


def finish_kernel(part_ref, couple_ref, keep_ref):
    own1 = part_ref[1] - mm6_rows(part_ref[2], couple_ref[...], NT)
    pack((part_ref[0], own1), keep_ref)


def mid_kernel(got_ref, out_ref):
    total = jnp.sum(got_ref[...], axis=0)
    per = 16
    rest = total[2 * per :]
    for s in range(2):
        out_ref[:, s, :] = total[s * per : (s + 1) * per]
        pieces = []
        for g in range(2):
            turn = (2 * s + g) * 32
            pieces.append(pltpu.roll(rest, LANES - turn, 1) if turn else rest)
        out_ref[:, 2 + s, :] = jnp.concatenate(pieces, axis=0)


def end_kernel(picks_ref, got_ref, weights_ref, out_ref):
    targets, rows = weights_ref.shape
    device, _, _ = place()
    total = jnp.sum(got_ref[...], axis=0)
    turned = jnp.transpose(jnp.concatenate([total, jnp.zeros((LANES - 4, LANES), jnp.float32)], axis=0))
    hot = onehots(picks_ref, device, rows)
    out_ref[:LANES, :] = weights_ref[:LANES, :] + (turned[:, 0:1] * hot[0:1] + turned[:, 1:2] * hot[1:2])
    left = targets - LANES
    out_ref[LANES:, :] = weights_ref[LANES:, :] + (
        turned[:left, 2:3] * hot[0:1] + turned[:left, 3:4] * hot[1:2]
    )


VMEM = pl.BlockSpec(memory_space=pltpu.VMEM)


def kernel(body, ins, outs, scratch=(), flops=0):
    single = not isinstance(outs, list)
    return pl.pallas_call(
        body,
        in_specs=ins,
        out_specs=VMEM if single else [VMEM] * len(outs),
        out_shape=outs,
        scratch_shapes=list(scratch),
        compiler_params=pltpu.CompilerParams(vmem_limit_bytes=VMEM_BYTES),
        cost_estimate=pl.CostEstimate(flops=flops, bytes_accessed=1 << 20, transcendentals=0),
    )


def f32(*dims):
    return jax.ShapeDtypeStruct(dims, jnp.float32)


def update(got, other, frames, weights, labels, picks, n_xy):
    half = got.shape[0]
    targets, rows = weights.shape
    tall = -(-targets // 8) * 8
    scratch = pltpu.VMEM((tall, rows), jnp.float32)
    known = kernel(
        own_kernel,
        [VMEM] * 5,
        [f32(2, half, half), f32(2, tall, half), f32(half, 2), f32(2, half)],
        [scratch, scratch],
        flops=6_000_000_000,
    )(picks, got, frames, weights, labels)
    send, part, couple = kernel(
        rest_kernel,
        [VMEM] * 8,
        [f32(n_xy, 40, LANES), f32(3, tall, half), f32(half, half)],
        [scratch],
        flops=6_000_000_000,
    )(got, other, frames, weights, *known)
    keep = kernel(finish_kernel, [VMEM] * 2, f32(n_xy, 40, LANES), flops=500_000_000)(part, couple)
    return keep, send


def shards(frames, labels, weights, picks):
    n_xy, n_z = lax.axis_size("xy"), lax.axis_size("z")
    frames, labels, weights = frames.T, labels.T, weights.T
    sent = pl.pallas_call(
        pick_kernel,
        grid=(1,),
        in_specs=[pl.BlockSpec(picks.shape, lambda i: (0, 0)), pl.BlockSpec(frames.shape, lambda i: (0, 0))],
        out_specs=pl.BlockSpec((n_z, 8, LANES), lambda i: (0, 0, 0)),
        out_shape=jax.ShapeDtypeStruct((n_z, 8, LANES), jnp.bfloat16),
        compiler_params=pltpu.CompilerParams(vmem_limit_bytes=60 * 1024 * 1024),
    )(picks, frames)
    got = lax.all_to_all(sent, "z", 0, 0).reshape(n_z, 8 * LANES)
    got = lax.all_to_all(jnp.broadcast_to(got[None], (n_xy,) + got.shape), "xy", 0, 0)
    got = got.reshape(n_xy * n_z, 8 * LANES)
    other = lax.ppermute(got, "core", [(0, 1), (1, 0)])
    keep, send = update(got, other, frames, weights, labels, picks, n_xy)
    got = lax.all_to_all(keep + lax.ppermute(send, "core", [(0, 1), (1, 0)]), "xy", 0, 0)
    part = kernel(mid_kernel, [VMEM], f32(n_z, 4, LANES))(got)
    got = lax.all_to_all(part, "z", 0, 0)
    return kernel(end_kernel, [VMEM] * 3, f32(*weights.shape))(picks, got, weights).T


def solution(mesh):
    grid = Mesh(mesh.devices.reshape(mesh.shape["row"], -1, 2), ("xy", "z", "core"))
    spread = P(("xy", "z", "core"), None)
    return jax.shard_map(
        shards, mesh=grid, in_specs=(spread, spread, spread, P()), out_specs=spread, check_vma=False
    )
```

```python
import jax
import jax.numpy as jnp
from jax import lax
from jax.experimental import pallas as pl
from jax.experimental.pallas import tpu as pltpu
from jax.sharding import Mesh, PartitionSpec as P

RIDGE = 1.0
LANES = 128
JOINT_STEPS = 4
VMEM_BYTES = 40 * 1024 * 1024

NN = (((1,), (0,)), ((), ()))
NT = (((1,), (1,)), ((), ()))


def mm(a, b, dims=NN):
    return lax.dot_general(a, b, dims, preferred_element_type=jnp.float32)


def split(a):
    hi = a.astype(jnp.bfloat16)
    lo = (a - hi.astype(jnp.float32)).astype(jnp.bfloat16)
    return hi, lo


def split3(a):
    hi = a.astype(jnp.bfloat16)
    rest = a - hi.astype(jnp.float32)
    mid = rest.astype(jnp.bfloat16)
    return hi, mid, (rest - mid.astype(jnp.float32)).astype(jnp.bfloat16)


def joined(left, right, dims):
    return mm(jnp.concatenate(left, axis=dims[0][0][0]), jnp.concatenate(right, axis=dims[0][1][0]), dims)


def mm3(a, b, dims=NN):
    return joined((a[0], a[1], a[0]), (b[0], b[0], b[1]), dims)


def split(a):
    hi = a.astype(jnp.bfloat16)
    lo = (a - hi.astype(jnp.float32)).astype(jnp.bfloat16)
    return hi, lo


def split3(a):
    hi = a.astype(jnp.bfloat16)
    rest = a - hi.astype(jnp.float32)
    mid = rest.astype(jnp.bfloat16)
    return hi, mid, (rest - mid.astype(jnp.float32)).astype(jnp.bfloat16)


def joined(left, right, dims):
    return mm(jnp.concatenate(left, axis=dims[0][0][0]), jnp.concatenate(right, axis=dims[0][1][0]), dims)


def mm3(a, b, dims=NN):
    return joined((a[0], a[1], a[0]), (b[0], b[0], b[1]), dims)


def mm6(a, b, dims=NN):
    a, b = split3(a), split3(b)
    return joined((a[0], a[1], a[2], a[0], a[1], a[0]), (b[0], b[0], b[0], b[1], b[1], b[2]), dims)


def mm6_rows(a, b, dims=NN):
    n = a.shape[0]
    a, b = split3(a), split3(b)
    p = mm(jnp.concatenate(a, axis=0), b[0], dims)
    q = mm(jnp.concatenate(a[:2], axis=0), b[1], dims)
    return p[:n] + (p[n : 2 * n] + q[:n]) + (p[2 * n :] + q[n:] + mm(a[0], b[2], dims))


def eye_mask(n):
    return lax.broadcasted_iota(jnp.int32, (n, n), 0) == lax.broadcasted_iota(jnp.int32, (n, n), 1)


def inverses(mats, others=()):
    others = list(others)

    def between():
        if others:
            others.pop(0)()

    n = mats[0].shape[0]
    eye = jnp.where(eye_mask(n), 1.0, 0.0).astype(jnp.float32)
    state = []
    for a in mats:
        top = jnp.max(jnp.sum(jnp.abs(a), axis=0, keepdims=True), axis=1, keepdims=True)
        top = jnp.maximum(top, 1.5)
        scale = 2.0 / (1.0 + top)
        err = (top - 1.0) / (top + 1.0)
        gain = 2.0 / (2.0 - err * err)
        r = eye - scale * a
        x = (gain * scale) * (eye + r)
        rs = split(r)
        r = (1.0 - gain) * eye + gain * mm3(rs, rs)
        state.append((x, r, err * err * gain * 0.5))
    between()
    for step in range(JOINT_STEPS + 1):
        later = []
        for x, r, err in state:
            gain = 2.0 / (2.0 - err * err)
            rs = split(r)
            x = gain * (x + joined(split(x), (rs[0], rs[0]), NN))
            if step < JOINT_STEPS:
                r = (1.0 - gain) * eye + gain * mm3(rs, rs)
            later.append((x, r, err * err * gain * 0.5))
        state = later
        between()
    exact = [eye - mm6(s[0], a) for a, s in zip(mats, state)]
    between()
    mid = []
    for r, (x, _, _) in zip(exact, state):
        rs = split(r)
        mid.append((x + mm3(rs, split(x)), mm(rs[0], rs[0])))
    between()
    out = [x + joined((r.astype(jnp.bfloat16),) * 2, split(x), NN) for x, r in mid]
    while others:
        between()
    return out


def place():
    xy, z, core = (lax.axis_index(a) for a in ("xy", "z", "core"))
    n_z, n_core = lax.axis_size("z"), lax.axis_size("core")
    return (xy * n_z + z) * n_core + core, xy * n_z + z, core


def onehots(picks_ref, device, rows):
    lane = lax.broadcasted_iota(jnp.int32, picks_ref.shape, 1)
    own = jnp.where(lane == device, picks_ref[...].astype(jnp.float32), 0.0)
    own = jnp.sum(own, axis=1, keepdims=True).astype(jnp.int32)
    return jnp.where(lax.broadcasted_iota(jnp.int32, (2, rows), 1) == own, 1.0, 0.0)


def pick_kernel(picks_ref, frames_ref, out_ref):
    feats, rows = frames_ref.shape
    device, _, _ = place()
    hot = onehots(picks_ref, device, rows)
    chosen = mm(hot.astype(jnp.bfloat16), frames_ref[...], NT)
    same = jnp.sum(hot[0:1] * hot[1:2], axis=1, keepdims=True)
    parts = []
    full = feats // LANES * LANES
    for s in range(2):
        parts += [chosen[s : s + 1, lo : lo + LANES] for lo in range(0, full, LANES)]
    gap = jnp.zeros((1, LANES // 2 - (feats - full)), jnp.float32)
    shared = jnp.concatenate([chosen[0:1, full:], gap, chosen[1:2, full:], gap], axis=1)
    lane = lax.broadcasted_iota(jnp.int32, (1, LANES), 1)
    parts += [jnp.where(lane == LANES - 1, same, shared), jnp.zeros((1, LANES), jnp.float32)]
    row = jnp.concatenate(parts, axis=0).astype(jnp.bfloat16)
    out_ref[...] = jnp.broadcast_to(row[None], out_ref.shape)


def halves(ref, feats):
    full = feats // LANES * LANES
    out = []
    for s in range(2):
        last = 2 * full + s * (LANES // 2)
        out.append(jnp.concatenate([ref[:, s * full : (s + 1) * full], ref[:, last : last + feats - full]], axis=1))
    return out


def gauss(tall, flat, inner, feats):
    return jnp.exp(-(tall + flat - 2.0 * inner) * (0.5 / feats))


def diag_sums(inner, diag):
    masked = jnp.where(diag, inner, 0.0)
    return jnp.sum(masked, axis=1, keepdims=True), jnp.sum(masked, axis=0, keepdims=True)


def term_of(chosen, tall, frames, frame_sq, wsplit, feats):
    near = gauss(tall, frame_sq, mm(chosen, frames), feats)
    return mm3(wsplit, split(near), NT)


def frame_squares(frames):
    wide = frames.astype(jnp.float32)
    return jnp.sum(wide * wide, axis=0, keepdims=True)


def padded(ref, scratch):
    scratch[...] = jnp.zeros_like(scratch)
    scratch[: ref.shape[0], :] = ref[...].astype(jnp.float32)
    return scratch[...]


def own_kernel(
    picks_ref, own_ref, frames_ref, weights_ref, labels_ref, inv_ref, term_ref, tall_ref, flat_ref, w_scr, l_scr
):
    feats, rows = frames_ref.shape
    half = own_ref.shape[0]
    device, pos, _ = place()
    chosen = halves(own_ref, feats)
    diag = eye_mask(half)
    one = jnp.where(diag, RIDGE, 0.0)
    inner = [mm(c, c, NT) for c in chosen]
    sums = [diag_sums(g, diag) for g in inner]
    mats = [gauss(t, f, g, feats) + one for (t, f), g in zip(sums, inner)]
    for s in range(2):
        flat_ref[s : s + 1, :] = sums[s][1]
        tall_ref[:, s : s + 1] = sums[s][0]
    kept = {}

    def prepare():
        kept["frames"] = frames_ref[...]
        kept["squares"] = frame_squares(kept["frames"])
        weights = padded(weights_ref, w_scr)
        kept["weights"] = split(weights)
        kept["start"] = padded(labels_ref, l_scr) - RIDGE * weights
        kept["hot"] = onehots(picks_ref, device, rows)

    def term(s):
        def go():
            here = lax.broadcasted_iota(jnp.int32, (1, half), 1) == pos
            picked = jnp.sum(kept["start"] * kept["hot"][s : s + 1], axis=1, keepdims=True)
            summed = term_of(chosen[s], sums[s][0], kept["frames"], kept["squares"], kept["weights"], feats)
            term_ref[s] = jnp.where(here, picked, 0.0) - summed

        return go

    inv = inverses(mats, [prepare, term(0), term(1)])
    for s in range(2):
        inv_ref[s] = inv[s]


def rest_kernel(
    own_ref, other_ref, frames_ref, weights_ref, inv_ref, term_ref, tall_ref, flat_ref, send_ref, part_ref, couple_ref, w_scr
):
    feats, rows = frames_ref.shape
    half = own_ref.shape[0]
    near = halves(own_ref, feats)
    far = halves(other_ref, feats)
    diag = eye_mask(half)
    one = jnp.where(diag, RIDGE, 0.0)
    inner = [mm(c, c, NT) for c in far]
    sums = [diag_sums(g, diag) for g in inner]
    talls = [[tall_ref[:, s : s + 1], sums[s][0]] for s in range(2)]
    flats = [[flat_ref[s : s + 1, :], sums[s][1]] for s in range(2)]
    chosen = [[near[s], far[s]] for s in range(2)]

    def block(s, i, t, j):
        return gauss(talls[s][i], flats[t][j], mm(chosen[s][i], chosen[t][j], NT), feats)

    inv = [inv_ref[s] for s in range(2)]
    upper = [block(s, 0, s, 1) for s in range(2)]
    lower, couple, schur = [], [], []
    for s in range(2):
        lower.append(block(s, 1, s, 0))
        couple.append(mm6_rows(inv[s], upper[s]))
    for s in range(2):
        corner = gauss(talls[s][1], flats[s][1], inner[s], feats) + one
        schur.append(corner - mm6_rows(lower[s], couple[s]))
    kept = {}

    def prepare():
        kept["frames"] = frames_ref[...]
        kept["squares"] = frame_squares(kept["frames"])
        kept["weights"] = split(padded(weights_ref, w_scr))

    def term(s):
        def go():
            kept["term", s] = -term_of(
                far[s], talls[s][1], kept["frames"], kept["squares"], kept["weights"], feats
            )

        return go

    def cross(i):
        def go():
            row = [block(1, i, 0, j) for j in range(2)]
            flag = (own_ref, other_ref)[i][:, -1:].astype(jnp.float32)
            row[i] = row[i] + jnp.where(diag, RIDGE * flag, 0.0)
            kept["cross", i] = jnp.concatenate(row, axis=1)

        return go

    def forward(s, first, second):
        return mm6_rows(first, inv[s]), second - mm6_rows(first, couple[s])

    def early():
        kept["forward"] = forward(0, term_ref[0], kept["term", 0])

    last = inverses(schur, [prepare, term(0), early, term(1), cross(0), cross(1)])

    y, m = kept["forward"]
    far0 = mm6_rows(m, last[0])
    own0 = y - mm6_rows(far0, couple[0], NT)
    both = jnp.concatenate([own0, far0], axis=1)
    first = term_ref[1] - mm6_rows(both, kept["cross", 0], NT)
    second = kept["term", 1] - mm6_rows(both, kept["cross", 1], NT)
    y, m = forward(1, first, second)
    far1 = mm6_rows(m, last[1])
    pack((far0, far1), send_ref)
    for i, part in enumerate((own0, y, far1)):
        part_ref[i] = part
    couple_ref[...] = couple[1]


def pack(deltas, out_ref):
    rows, half = deltas[0].shape
    per = 16
    groups = half // per
    fill = jnp.zeros((2 * LANES - rows, half), jnp.float32)
    packed = None
    for s in range(2):
        full = jnp.concatenate([deltas[s], fill], axis=0)
        out_ref[:, s * per : (s + 1) * per, :] = jnp.transpose(full[:LANES]).reshape(groups, per, LANES)
        tail = jnp.transpose(full[LANES:]).reshape(groups, 2, 8, LANES)
        for g in range(2):
            piece = tail[:, g].reshape(groups * 8, LANES)
            turn = (2 * s + g) * 32
            if turn:
                piece = pltpu.roll(piece, turn, 1)
            packed = piece if packed is None else packed + piece
    out_ref[:, 2 * per :, :] = packed.reshape(groups, 8, LANES)


def finish_kernel(part_ref, couple_ref, keep_ref):
    own1 = part_ref[1] - mm6_rows(part_ref[2], couple_ref[...], NT)
    pack((part_ref[0], own1), keep_ref)


def mid_kernel(got_ref, out_ref):
    total = jnp.sum(got_ref[...], axis=0)
    per = 16
    rest = total[2 * per :]
    for s in range(2):
        out_ref[:, s, :] = total[s * per : (s + 1) * per]
        pieces = []
        for g in range(2):
            turn = (2 * s + g) * 32
            pieces.append(pltpu.roll(rest, LANES - turn, 1) if turn else rest)
        out_ref[:, 2 + s, :] = jnp.concatenate(pieces, axis=0)


def end_kernel(picks_ref, got_ref, weights_ref, out_ref):
    targets, rows = weights_ref.shape
    device, _, _ = place()
    total = jnp.sum(got_ref[...], axis=0)
    turned = jnp.transpose(jnp.concatenate([total, jnp.zeros((LANES - 4, LANES), jnp.float32)], axis=0))
    hot = onehots(picks_ref, device, rows)
    out_ref[:LANES, :] = weights_ref[:LANES, :] + (turned[:, 0:1] * hot[0:1] + turned[:, 1:2] * hot[1:2])
    left = targets - LANES
    out_ref[LANES:, :] = weights_ref[LANES:, :] + (
        turned[:left, 2:3] * hot[0:1] + turned[:left, 3:4] * hot[1:2]
    )


VMEM = pl.BlockSpec(memory_space=pltpu.VMEM)


def kernel(body, ins, outs, scratch=(), flops=0):
    single = not isinstance(outs, list)
    return pl.pallas_call(
        body,
        in_specs=ins,
        out_specs=VMEM if single else [VMEM] * len(outs),
        out_shape=outs,
        scratch_shapes=list(scratch),
        compiler_params=pltpu.CompilerParams(vmem_limit_bytes=VMEM_BYTES),
        cost_estimate=pl.CostEstimate(flops=flops, bytes_accessed=1 << 20, transcendentals=0),
    )


def f32(*dims):
    return jax.ShapeDtypeStruct(dims, jnp.float32)


def update(got, other, frames, weights, labels, picks, n_xy):
    half = got.shape[0]
    targets, rows = weights.shape
    tall = -(-targets // 8) * 8
    scratch = pltpu.VMEM((tall, rows), jnp.float32)
    known = kernel(
        own_kernel,
        [VMEM] * 5,
        [f32(2, half, half), f32(2, tall, half), f32(half, 2), f32(2, half)],
        [scratch, scratch],
        flops=6_000_000_000,
    )(picks, got, frames, weights, labels)
    send, part, couple = kernel(
        rest_kernel,
        [VMEM] * 8,
        [f32(n_xy, 40, LANES), f32(3, tall, half), f32(half, half)],
        [scratch],
        flops=6_000_000_000,
    )(got, other, frames, weights, *known)
    keep = kernel(finish_kernel, [VMEM] * 2, f32(n_xy, 40, LANES), flops=500_000_000)(part, couple)
    return keep, send


def shards(frames, labels, weights, picks):
    n_xy, n_z = lax.axis_size("xy"), lax.axis_size("z")
    frames, labels, weights = frames.T, labels.T, weights.T
    sent = pl.pallas_call(
        pick_kernel,
        grid=(1,),
        in_specs=[pl.BlockSpec(picks.shape, lambda i: (0, 0)), pl.BlockSpec(frames.shape, lambda i: (0, 0))],
        out_specs=pl.BlockSpec((n_z, 8, LANES), lambda i: (0, 0, 0)),
        out_shape=jax.ShapeDtypeStruct((n_z, 8, LANES), jnp.bfloat16),
        compiler_params=pltpu.CompilerParams(vmem_limit_bytes=60 * 1024 * 1024),
    )(picks, frames)
    got = lax.all_to_all(sent, "z", 0, 0).reshape(n_z, 8 * LANES)[:, : 7 * LANES]
    got = lax.all_to_all(jnp.broadcast_to(got[None], (n_xy,) + got.shape), "xy", 0, 0)
    got = got.reshape(n_xy * n_z, 7 * LANES)
    other = lax.ppermute(got, "core", [(0, 1), (1, 0)])
    keep, send = update(got, other, frames, weights, labels, picks, n_xy)
    got = lax.all_to_all(keep + lax.ppermute(send, "core", [(0, 1), (1, 0)]), "xy", 0, 0)
    part = kernel(mid_kernel, [VMEM], f32(n_z, 4, LANES))(got)
    got = lax.all_to_all(part, "z", 0, 0)
    return kernel(end_kernel, [VMEM] * 3, f32(*weights.shape))(picks, got, weights).T


def solution(mesh):
    grid = Mesh(mesh.devices.reshape(mesh.shape["row"], -1, 2), ("xy", "z", "core"))
    spread = P(("xy", "z", "core"), None)
    return jax.shard_map(
        shards, mesh=grid, in_specs=(spread, spread, spread, P()), out_specs=spread, check_vma=False
    )
```

```python
import jax
import jax.numpy as jnp
from jax import lax
from jax.experimental import pallas as pl
from jax.experimental.pallas import tpu as pltpu
from jax.sharding import Mesh, PartitionSpec as P

RIDGE = 1.0
LANES = 128
JOINT_STEPS = 4
VMEM_BYTES = 40 * 1024 * 1024

NN = (((1,), (0,)), ((), ()))
NT = (((1,), (1,)), ((), ()))


def mm(a, b, dims=NN):
    return lax.dot_general(a, b, dims, preferred_element_type=jnp.float32)


def split(a):
    hi = a.astype(jnp.bfloat16)
    lo = (a - hi.astype(jnp.float32)).astype(jnp.bfloat16)
    return hi, lo


def split3(a):
    hi = a.astype(jnp.bfloat16)
    rest = a - hi.astype(jnp.float32)
    mid = rest.astype(jnp.bfloat16)
    return hi, mid, (rest - mid.astype(jnp.float32)).astype(jnp.bfloat16)


def joined(left, right, dims):
    return mm(jnp.concatenate(left, axis=dims[0][0][0]), jnp.concatenate(right, axis=dims[0][1][0]), dims)


def mm3(a, b, dims=NN):
    return joined((a[0], a[1], a[0]), (b[0], b[0], b[1]), dims)


def split(a):
    hi = a.astype(jnp.bfloat16)
    lo = (a - hi.astype(jnp.float32)).astype(jnp.bfloat16)
    return hi, lo


def split3(a):
    hi = a.astype(jnp.bfloat16)
    rest = a - hi.astype(jnp.float32)
    mid = rest.astype(jnp.bfloat16)
    return hi, mid, (rest - mid.astype(jnp.float32)).astype(jnp.bfloat16)


def joined(left, right, dims):
    return mm(jnp.concatenate(left, axis=dims[0][0][0]), jnp.concatenate(right, axis=dims[0][1][0]), dims)


def mm3(a, b, dims=NN):
    return joined((a[0], a[1], a[0]), (b[0], b[0], b[1]), dims)


def mm6(a, b, dims=NN):
    a, b = split3(a), split3(b)
    return joined((a[0], a[1], a[2], a[0], a[1], a[0]), (b[0], b[0], b[0], b[1], b[1], b[2]), dims)


def mm6_rows(a, b, dims=NN):
    n = a.shape[0]
    a, b = split3(a), split3(b)
    p = mm(jnp.concatenate(a, axis=0), b[0], dims)
    q = mm(jnp.concatenate(a[:2], axis=0), b[1], dims)
    return p[:n] + (p[n : 2 * n] + q[:n]) + (p[2 * n :] + q[n:] + mm(a[0], b[2], dims))


def eye_mask(n):
    return lax.broadcasted_iota(jnp.int32, (n, n), 0) == lax.broadcasted_iota(jnp.int32, (n, n), 1)


def inverses(mats, others=()):
    others = list(others)

    def between():
        if others:
            others.pop(0)()

    n = mats[0].shape[0]
    eye = jnp.where(eye_mask(n), 1.0, 0.0).astype(jnp.float32)
    state = []
    for a in mats:
        top = jnp.max(jnp.sum(jnp.abs(a), axis=0, keepdims=True), axis=1, keepdims=True)
        top = jnp.maximum(top, 1.5)
        scale = 2.0 / (1.0 + top)
        err = (top - 1.0) / (top + 1.0)
        gain = 2.0 / (2.0 - err * err)
        r = eye - scale * a
        x = (gain * scale) * (eye + r)
        rs = split(r)
        r = (1.0 - gain) * eye + gain * mm3(rs, rs)
        state.append((x, r, err * err * gain * 0.5))
    between()
    for step in range(JOINT_STEPS + 1):
        later = []
        for x, r, err in state:
            gain = 2.0 / (2.0 - err * err)
            rs = split(r)
            x = gain * (x + joined(split(x), (rs[0], rs[0]), NN))
            if step < JOINT_STEPS:
                r = (1.0 - gain) * eye + gain * mm3(rs, rs)
            later.append((x, r, err * err * gain * 0.5))
        state = later
        between()
    exact = [eye - mm6(s[0], a) for a, s in zip(mats, state)]
    between()
    mid = []
    for r, (x, _, _) in zip(exact, state):
        rs = split(r)
        mid.append((x + mm3(rs, split(x)), mm(rs[0], rs[0])))
    between()
    out = [x + joined((r.astype(jnp.bfloat16),) * 2, split(x), NN) for x, r in mid]
    while others:
        between()
    return out


def place():
    xy, z, core = (lax.axis_index(a) for a in ("xy", "z", "core"))
    n_z, n_core = lax.axis_size("z"), lax.axis_size("core")
    return (xy * n_z + z) * n_core + core, xy * n_z + z, core


def onehots(picks_ref, device, rows):
    lane = lax.broadcasted_iota(jnp.int32, picks_ref.shape, 1)
    own = jnp.where(lane == device, picks_ref[...].astype(jnp.float32), 0.0)
    own = jnp.sum(own, axis=1, keepdims=True).astype(jnp.int32)
    return jnp.where(lax.broadcasted_iota(jnp.int32, (2, rows), 1) == own, 1.0, 0.0)


def pick_kernel(picks_ref, frames_ref, out_ref):
    feats, rows = frames_ref.shape
    device, _, _ = place()
    hot = onehots(picks_ref, device, rows)
    chosen = mm(hot.astype(jnp.bfloat16), frames_ref[...], NT)
    same = jnp.sum(hot[0:1] * hot[1:2], axis=1, keepdims=True)
    lane = lax.broadcasted_iota(jnp.int32, (1, LANES), 1)
    parts = []
    for s in range(2):
        for c in range(4):
            lo = c * LANES
            wide = min(LANES, feats - lo)
            piece = chosen[s : s + 1, lo : lo + wide]
            if wide < LANES:
                piece = jnp.concatenate([piece, jnp.zeros((1, LANES - wide), jnp.float32)], axis=1)
                piece = jnp.where(lane == wide, same, piece)
            parts.append(piece)
    row = jnp.concatenate(parts, axis=0).astype(jnp.bfloat16)
    out_ref[...] = jnp.broadcast_to(row[None], out_ref.shape)


def halves(ref, feats):
    width = ref.shape[1] // 2
    return [ref[:, s * width : s * width + feats] for s in range(2)]


def gauss(tall, flat, inner, feats):
    return jnp.exp(-(tall + flat - 2.0 * inner) * (0.5 / feats))


def diag_sums(inner, diag):
    masked = jnp.where(diag, inner, 0.0)
    return jnp.sum(masked, axis=1, keepdims=True), jnp.sum(masked, axis=0, keepdims=True)


def term_of(chosen, tall, frames, frame_sq, wsplit, feats):
    near = gauss(tall, frame_sq, mm(chosen, frames), feats)
    return mm3(wsplit, split(near), NT)


def frame_squares(frames):
    wide = frames.astype(jnp.float32)
    return jnp.sum(wide * wide, axis=0, keepdims=True)


def padded(ref, scratch):
    scratch[...] = jnp.zeros_like(scratch)
    scratch[: ref.shape[0], :] = ref[...].astype(jnp.float32)
    return scratch[...]


def own_kernel(
    picks_ref, own_ref, frames_ref, weights_ref, labels_ref, inv_ref, term_ref, tall_ref, flat_ref, w_scr, l_scr
):
    feats, rows = frames_ref.shape
    half = own_ref.shape[0]
    device, pos, _ = place()
    chosen = halves(own_ref, feats)
    diag = eye_mask(half)
    one = jnp.where(diag, RIDGE, 0.0)
    inner = [mm(c, c, NT) for c in chosen]
    sums = [diag_sums(g, diag) for g in inner]
    mats = [gauss(t, f, g, feats) + one for (t, f), g in zip(sums, inner)]
    for s in range(2):
        flat_ref[s : s + 1, :] = sums[s][1]
        tall_ref[:, s : s + 1] = sums[s][0]
    kept = {}

    def prepare():
        kept["frames"] = frames_ref[...]
        kept["squares"] = frame_squares(kept["frames"])
        weights = padded(weights_ref, w_scr)
        kept["weights"] = split(weights)
        kept["start"] = padded(labels_ref, l_scr) - RIDGE * weights
        kept["hot"] = onehots(picks_ref, device, rows)

    def term(s):
        def go():
            here = lax.broadcasted_iota(jnp.int32, (1, half), 1) == pos
            picked = jnp.sum(kept["start"] * kept["hot"][s : s + 1], axis=1, keepdims=True)
            summed = term_of(chosen[s], sums[s][0], kept["frames"], kept["squares"], kept["weights"], feats)
            term_ref[s] = jnp.where(here, picked, 0.0) - summed

        return go

    inv = inverses(mats, [prepare, term(0), term(1)])
    for s in range(2):
        inv_ref[s] = inv[s]


def rest_kernel(
    own_ref, other_ref, frames_ref, weights_ref, inv_ref, term_ref, tall_ref, flat_ref, send_ref, part_ref, couple_ref, w_scr
):
    feats, rows = frames_ref.shape
    half = own_ref.shape[0]
    width = own_ref.shape[1] // 2
    near = halves(own_ref, feats)
    far = halves(other_ref, feats)
    diag = eye_mask(half)
    one = jnp.where(diag, RIDGE, 0.0)
    inner = [mm(c, c, NT) for c in far]
    sums = [diag_sums(g, diag) for g in inner]
    talls = [[tall_ref[:, s : s + 1], sums[s][0]] for s in range(2)]
    flats = [[flat_ref[s : s + 1, :], sums[s][1]] for s in range(2)]
    chosen = [[near[s], far[s]] for s in range(2)]

    def block(s, i, t, j):
        return gauss(talls[s][i], flats[t][j], mm(chosen[s][i], chosen[t][j], NT), feats)

    inv = [inv_ref[s] for s in range(2)]
    upper = [block(s, 0, s, 1) for s in range(2)]
    couple, schur = [], []
    for s in range(2):
        couple.append(mm6_rows(inv[s], upper[s]))
    for s in range(2):
        corner = gauss(talls[s][1], flats[s][1], inner[s], feats) + one
        schur.append(corner - mm6_rows(jnp.transpose(upper[s]), couple[s]))
    kept = {}

    def prepare():
        kept["frames"] = frames_ref[...]
        kept["squares"] = frame_squares(kept["frames"])
        kept["weights"] = split(padded(weights_ref, w_scr))

    def term(s):
        def go():
            kept["term", s] = -term_of(
                far[s], talls[s][1], kept["frames"], kept["squares"], kept["weights"], feats
            )

        return go

    def cross(i):
        def go():
            row = [block(1, i, 0, j) for j in range(2)]
            flag = (own_ref, other_ref)[i][:, width + feats : width + feats + 1].astype(jnp.float32)
            row[i] = row[i] + jnp.where(diag, RIDGE * flag, 0.0)
            kept["cross", i] = jnp.concatenate(row, axis=1)

        return go

    def forward(s, first, second):
        return mm6_rows(first, inv[s]), second - mm6_rows(first, couple[s])

    def early():
        kept["forward"] = forward(0, term_ref[0], kept["term", 0])

    last = inverses(schur, [prepare, term(0), early, term(1), cross(0), cross(1)])

    y, m = kept["forward"]
    far0 = mm6_rows(m, last[0])
    own0 = y - mm6_rows(far0, couple[0], NT)
    both = jnp.concatenate([own0, far0], axis=1)
    first = term_ref[1] - mm6_rows(both, kept["cross", 0], NT)
    second = kept["term", 1] - mm6_rows(both, kept["cross", 1], NT)
    y, m = forward(1, first, second)
    far1 = mm6_rows(m, last[1])
    pack((far0, far1), send_ref)
    for i, part in enumerate((own0, y, far1)):
        part_ref[i] = part
    couple_ref[...] = couple[1]


def pack(deltas, out_ref):
    rows, half = deltas[0].shape
    per = 16
    groups = half // per
    fill = jnp.zeros((2 * LANES - rows, half), jnp.float32)
    packed = None
    for s in range(2):
        full = jnp.concatenate([deltas[s], fill], axis=0)
        out_ref[:, s * per : (s + 1) * per, :] = jnp.transpose(full[:LANES]).reshape(groups, per, LANES)
        tail = jnp.transpose(full[LANES:]).reshape(groups, 2, 8, LANES)
        for g in range(2):
            piece = tail[:, g].reshape(groups * 8, LANES)
            turn = (2 * s + g) * 32
            if turn:
                piece = pltpu.roll(piece, turn, 1)
            packed = piece if packed is None else packed + piece
    out_ref[:, 2 * per :, :] = packed.reshape(groups, 8, LANES)


def finish_kernel(part_ref, couple_ref, keep_ref):
    own1 = part_ref[1] - mm6_rows(part_ref[2], couple_ref[...], NT)
    pack((part_ref[0], own1), keep_ref)


def mid_kernel(got_ref, out_ref):
    total = jnp.sum(got_ref[...], axis=0)
    per = 16
    rest = total[2 * per :]
    for s in range(2):
        out_ref[:, s, :] = total[s * per : (s + 1) * per]
        pieces = []
        for g in range(2):
            turn = (2 * s + g) * 32
            pieces.append(pltpu.roll(rest, LANES - turn, 1) if turn else rest)
        out_ref[:, 2 + s, :] = jnp.concatenate(pieces, axis=0)


def end_kernel(picks_ref, got_ref, weights_ref, out_ref):
    targets, rows = weights_ref.shape
    device, _, _ = place()
    total = jnp.sum(got_ref[...], axis=0)
    turned = jnp.transpose(jnp.concatenate([total, jnp.zeros((LANES - 4, LANES), jnp.float32)], axis=0))
    hot = onehots(picks_ref, device, rows)
    out_ref[:LANES, :] = weights_ref[:LANES, :] + (turned[:, 0:1] * hot[0:1] + turned[:, 1:2] * hot[1:2])
    left = targets - LANES
    out_ref[LANES:, :] = weights_ref[LANES:, :] + (
        turned[:left, 2:3] * hot[0:1] + turned[:left, 3:4] * hot[1:2]
    )


VMEM = pl.BlockSpec(memory_space=pltpu.VMEM)


def kernel(body, ins, outs, scratch=(), flops=0):
    single = not isinstance(outs, list)
    return pl.pallas_call(
        body,
        in_specs=ins,
        out_specs=VMEM if single else [VMEM] * len(outs),
        out_shape=outs,
        scratch_shapes=list(scratch),
        compiler_params=pltpu.CompilerParams(vmem_limit_bytes=VMEM_BYTES),
        cost_estimate=pl.CostEstimate(flops=flops, bytes_accessed=1 << 20, transcendentals=0),
    )


def f32(*dims):
    return jax.ShapeDtypeStruct(dims, jnp.float32)


def update(got, other, frames, weights, labels, picks, n_xy):
    half = got.shape[0]
    targets, rows = weights.shape
    tall = -(-targets // 8) * 8
    scratch = pltpu.VMEM((tall, rows), jnp.float32)
    known = kernel(
        own_kernel,
        [VMEM] * 5,
        [f32(2, half, half), f32(2, tall, half), f32(half, 2), f32(2, half)],
        [scratch, scratch],
        flops=6_000_000_000,
    )(picks, got, frames, weights, labels)
    send, part, couple = kernel(
        rest_kernel,
        [VMEM] * 8,
        [f32(n_xy, 40, LANES), f32(3, tall, half), f32(half, half)],
        [scratch],
        flops=6_000_000_000,
    )(got, other, frames, weights, *known)
    keep = kernel(finish_kernel, [VMEM] * 2, f32(n_xy, 40, LANES), flops=500_000_000)(part, couple)
    return keep, send


def shards(frames, labels, weights, picks):
    n_xy, n_z = lax.axis_size("xy"), lax.axis_size("z")
    frames, labels, weights = frames.T, labels.T, weights.T
    sent = pl.pallas_call(
        pick_kernel,
        grid=(1,),
        in_specs=[pl.BlockSpec(picks.shape, lambda i: (0, 0)), pl.BlockSpec(frames.shape, lambda i: (0, 0))],
        out_specs=pl.BlockSpec((n_z, 8, LANES), lambda i: (0, 0, 0)),
        out_shape=jax.ShapeDtypeStruct((n_z, 8, LANES), jnp.bfloat16),
        compiler_params=pltpu.CompilerParams(vmem_limit_bytes=60 * 1024 * 1024),
    )(picks, frames)
    got = lax.all_to_all(sent, "z", 0, 0).reshape(n_z, 8 * LANES)
    got = lax.all_to_all(jnp.broadcast_to(got[None], (n_xy,) + got.shape), "xy", 0, 0)
    got = got.reshape(n_xy * n_z, 8 * LANES)
    other = lax.ppermute(got, "core", [(0, 1), (1, 0)])
    keep, send = update(got, other, frames, weights, labels, picks, n_xy)
    got = lax.all_to_all(keep + lax.ppermute(send, "core", [(0, 1), (1, 0)]), "xy", 0, 0)
    part = kernel(mid_kernel, [VMEM], f32(n_z, 4, LANES))(got)
    got = lax.all_to_all(part, "z", 0, 0)
    return kernel(end_kernel, [VMEM] * 3, f32(*weights.shape))(picks, got, weights).T


def solution(mesh):
    grid = Mesh(mesh.devices.reshape(mesh.shape["row"], -1, 2), ("xy", "z", "core"))
    spread = P(("xy", "z", "core"), None)
    return jax.shard_map(
        shards, mesh=grid, in_specs=(spread, spread, spread, P()), out_specs=spread, check_vma=False
    )
```
